128 devices in a mesh: dp: 8 (over y, z_hi), ctx: 16 (over x, z_lo, core).
Axes of the slice: x: 4, y: 4, z: 4 (z_hi: 2, z_lo: 2; z = z_hi * 2 + z_lo), core: 2. Of those that a mesh axis runs over, the one named last changes fastest.
Arguments:
- inputs: bfloat16 [8, 2048, 4096], P('dp', 'ctx'), may hold values from -8 to 8
- queries: bfloat16 [8, 2048, 8192], P('dp', 'ctx'), may hold values from -256 to 256
- grad_output: bfloat16 [8, 2048, 8192], P('dp', 'ctx'), may hold values from -6 to 6
- kv_weight: bfloat16 [4096, 1024], P(('dp', 'ctx')), may hold values from -1 to 1
Outputs:
- attn_out: bfloat16 [8, 2048, 8192], P('dp', 'ctx')
- grad_query: bfloat16 [8, 2048, 8192], P('dp', 'ctx')
- grad_inputs: bfloat16 [8, 2048, 4096], P('dp', 'ctx')
- grad_weight: float32 [4096, 1024], P(('dp', 'ctx'))
The draws below stay inside these ranges and needn't reach their ends.
All inputs are finite; a program needn't handle non-finite values.
Results may differ from the reference program's by a relative error of at most 0.035.
Values may be sent and summed in bfloat16 or wider, within the bound.
A program may use at most 128 MiB of HBM per device.

```python
import jax
import jax.numpy as jnp
from jax import lax

D = 4096
HQ = 64
KVH = 4
DH = 128
SEQLEN = 2048
SEQS = 8


def input_field(key):
    normal_key = jax.random.fold_in(key, 101)
    field = jax.random.normal(normal_key, (SEQS, SEQLEN, D), jnp.float32)
    return jnp.clip(field, -8.0, 8.0)


def weight_field(key):
    normal_key = jax.random.fold_in(key, 201)
    field = jax.random.normal(normal_key, (D, 2 * KVH * DH), jnp.float32)
    return jnp.clip(field, -2.5, 2.5) * D ** (-0.5)


def draw_inputs(key, part):
    return input_field(key).astype(jnp.bfloat16)


def draw_kv_weight(key, part):
    return weight_field(key).astype(jnp.bfloat16)


def draw_queries(key, part):
    base_key = jax.random.fold_in(key, 301)
    field = jnp.clip(jax.random.normal(base_key, (SEQS, SEQLEN, HQ * DH), jnp.float32), -6.0, 6.0)
    return field.astype(jnp.bfloat16)


def shard_levels(own_key, dims, cuts, low, top_value):
    def one(position, shards_of):
        draws = jax.random.uniform(jax.random.fold_in(jax.random.fold_in(own_key, 6), position), (shards_of,), jnp.float32, low / len(cuts), top_value / len(cuts))
        return jnp.repeat(jnp.exp(draws), dims[position] // shards_of).reshape((-1,) + (1,) * (len(dims) - position - 1))

    loudness = one(*cuts[0])
    for cut in cuts[1:]:
        loudness = loudness * one(*cut)
    return loudness


def gaussian(rng, shape, spread, most, split=(), kind=jnp.bfloat16):
    values = jax.random.normal(rng, shape, jnp.float32) * spread
    if len(split) > 0:
        values = shard_levels(rng, shape, split, -0.22, 0.18) * values
    return jnp.clip(values, min=-most, max=most).astype(kind)


def setup_inputs(seed: int = 0) -> dict:
    splits = jax.random.split(jax.random.key(seed), 5)
    inputs = draw_inputs(jax.random.fold_in(splits[4], 71), 0)
    queries = draw_queries(jax.random.fold_in(splits[4], 71), 0)
    grad_output = gaussian(splits[2], (SEQS, SEQLEN, HQ * DH), 1.0, 6.0, ((0, 8), (1, 16)))
    kv_weight = draw_kv_weight(jax.random.fold_in(splits[4], 71), 0)
    return dict(inputs=inputs, queries=queries, grad_output=grad_output, kv_weight=kv_weight)


ROPE_BASE = 500000.0


def rope_tables(positions, head_dim):
    half_dim = head_dim // 2
    frequency = ROPE_BASE ** (-2.0 * jnp.arange(half_dim, dtype=jnp.float32) / head_dim)
    angles = positions.astype(jnp.float32)[:, None] * frequency[None, :]
    return jnp.cos(angles)[:, None, :], jnp.sin(angles)[:, None, :]


def rotary(values, positions):
    half_dim = values.shape[-1] // 2
    cosine, sine_table = rope_tables(positions, values.shape[-1])
    first_half = values[..., :half_dim]
    second = values[..., half_dim:]
    return jnp.concatenate([first_half * cosine - second * sine_table, second * cosine + first_half * sine_table], axis=-1)


def rotary_back(gradient, positions):
    half_dim = gradient.shape[-1] // 2
    cosine, sine_table = rope_tables(positions, gradient.shape[-1])
    first_half = gradient[..., :half_dim]
    second = gradient[..., half_dim:]
    return jnp.concatenate([first_half * cosine + second * sine_table, second * cosine - first_half * sine_table], axis=-1)


def rounded(operand):
    return lax.optimization_barrier(operand.astype(jnp.bfloat16)).astype(jnp.float32)


def one_sequence(inputs_seq, query_seq, grad_seq, kv_weight):
    length = inputs_seq.shape[0]
    half_cols = KVH * DH
    group_size = HQ // KVH
    projected = jnp.dot(inputs_seq, kv_weight, preferred_element_type=jnp.float32)
    positions = jnp.arange(length, dtype=jnp.int32)
    key_rows = rotary(projected[:, :half_cols].reshape(length, KVH, DH), positions).astype(jnp.bfloat16)
    value_rows = projected[:, half_cols:].reshape(length, KVH, DH).astype(jnp.bfloat16)
    queries = query_seq.reshape(length, KVH, group_size, DH).astype(jnp.float32)
    cotangent = grad_seq.reshape(length, KVH, group_size, DH).astype(jnp.float32)
    causal = positions[:, None] >= positions[None, :]
    score_scale = DH ** -0.5
    outs_heads = []
    grad_q_heads = []
    grad_k_heads = []
    grad_v_heads = []
    for head_index in range(KVH):
        query_head = queries[:, head_index]
        key_head = key_rows[:, head_index].astype(jnp.float32)
        value_head = value_rows[:, head_index].astype(jnp.float32)
        grad_head = cotangent[:, head_index]
        scores = jnp.einsum("qgd,kd->gqk", query_head, key_head) * score_scale
        scores = jnp.where(causal[None], scores, -jnp.inf)
        row_top = jnp.max(scores, axis=-1, keepdims=True)
        weights = jnp.exp(scores - row_top)
        row_total = jnp.sum(weights, axis=-1, keepdims=True)
        weighted = jnp.einsum("gqk,kd->gqd", rounded(weights), value_head) / row_total
        attn_rounded = lax.optimization_barrier(jnp.transpose(weighted, (1, 0, 2)).astype(jnp.bfloat16))
        log_total = row_top + jnp.log(row_total)
        row_delta = jnp.sum(grad_head * attn_rounded.astype(jnp.float32), axis=-1)
        probs_now = jnp.exp(scores - log_total)
        dprobs = jnp.einsum("qgd,kd->gqk", grad_head, value_head)
        dscores = probs_now * (dprobs - jnp.transpose(row_delta)[:, :, None])
        dscores_b = rounded(dscores)
        grad_q_heads.append((jnp.einsum("gqk,kd->qgd", dscores_b, key_head) * score_scale).astype(jnp.bfloat16))
        grad_k_heads.append(jnp.einsum("gqk,qgd->kd", dscores_b, query_head) * score_scale)
        grad_v_heads.append(jnp.einsum("gqk,qgd->kd", rounded(probs_now), grad_head))
        outs_heads.append(attn_rounded)
    attn_out = jnp.stack(outs_heads, axis=1).reshape(length, HQ * DH)
    grad_query = jnp.stack(grad_q_heads, axis=1).reshape(length, HQ * DH)
    grad_keys = jnp.stack(grad_k_heads, axis=1)
    grad_values = jnp.stack(grad_v_heads, axis=1)
    grad_projected = jnp.concatenate([rotary_back(grad_keys, positions).reshape(length, half_cols), grad_values.reshape(length, half_cols)], axis=1).astype(jnp.bfloat16)
    grad_inputs = jnp.dot(grad_projected, kv_weight.T, preferred_element_type=jnp.float32).astype(jnp.bfloat16)
    grad_weight = jnp.dot(inputs_seq.T, grad_projected, preferred_element_type=jnp.float32)
    return attn_out, grad_query, grad_inputs, grad_weight


def reference(inputs, queries, grad_output, kv_weight):
    def per_sequence(operands):
        return one_sequence(operands[0], operands[1], operands[2], kv_weight)

    attn_out, grad_query, grad_inputs, grad_parts = lax.map(per_sequence, (inputs, queries, grad_output))
    return attn_out, grad_query, grad_inputs, jnp.sum(grad_parts, axis=0)
```

```python
import functools
import math

import jax
import jax.numpy as jnp
from jax import lax
from jax.experimental import pallas as pl
from jax.experimental.pallas import tpu as pltpu
from jax.sharding import PartitionSpec as P

DH = 128
LOG2E = math.log2(math.e)
ROPE_BASE = 500000.0
MESH = pl.DeviceIdType.MESH
NDP, NCTX = 8, 16
CHIPS = NCTX // 2
f32, bf16 = jnp.float32, jnp.bfloat16


def rope_tables(positions, head_dim):
    half_dim = head_dim // 2
    frequency = ROPE_BASE ** (-2.0 * jnp.arange(half_dim, dtype=f32) / head_dim)
    angles = positions.astype(f32)[:, None] * frequency[None, :]
    return (jnp.cos(angles)[:, None, :], jnp.sin(angles)[:, None, :])


def rotary(values, tables, sign):
    half_dim = values.shape[-1] // 2
    cosine, sine = tables
    a = values[..., :half_dim]
    b = values[..., half_dim:]
    return jnp.concatenate([a * cosine - sign * b * sine, b * cosine + sign * a * sine], axis=-1)


def position():
    dp, ctx = lax.axis_index("dp"), lax.axis_index("ctx")
    return dp // 2, dp % 2, ctx // 4, (ctx // 2) % 2, ctx % 2


def device_at(y, zh, x, zl, core):
    return (y * 2 + zh, x * 4 + zl * 2 + core)


def meet(peers):
    barrier = pltpu.get_barrier_semaphore()
    for peer in peers:
        pl.semaphore_signal(barrier, inc=1, device_id=peer, device_id_type=MESH)
    pl.semaphore_wait(barrier, len(peers))


PARTS = ((0, 384, "zyx"), (384, 384, "yxz"), (768, 256, "xzy"))


def gather_weight_kernel(w_ref, out_ref, own_sem, send, recv, core_send, core_recv):
    y, zh, x, zl, core = position()
    z = zh * 2 + zl

    def peer(axis, step):
        if axis == "x":
            return device_at(y, zh, lax.rem(x + step, 4), zl, core)
        if axis == "y":
            return device_at(lax.rem(y + step, 4), zh, x, zl, core)
        far = lax.rem(z + step, 4)
        return device_at(y, far // 2, x, lax.rem(far, 2), core)

    partner = device_at(y, zh, x, zl, 1 - core)
    meet([peer(axis, step) for axis in "xyz" for step in (1, 2, 3)] + [partner])

    def region(done, start, width):
        yy = slice(None) if "y" in done else y
        xx = slice(None) if "x" in done else x
        zz = slice(None) if "z" in done else z
        return out_ref.at[yy, zz, xx, core, :, pl.ds(start, width)]

    own = pltpu.make_async_copy(w_ref, out_ref.at[y, z, x, core], own_sem)
    own.start()
    own.wait()
    waits = []

    def push(part, phase):
        start, width, order = PARTS[part]
        src = region(order[:phase], start, width)
        copies = []
        for step in (1, 2, 3):
            k = (part * 3 + phase) * 3 + step - 1
            cp = pltpu.make_async_remote_copy(
                src_ref=src, dst_ref=src, send_sem=send.at[k], recv_sem=recv.at[k],
                device_id=peer(order[phase], step), device_id_type=MESH)
            cp.start()
            copies.append(cp)
        return copies

    for phase in range(3):
        current = [push(part, phase) for part in range(3)]
        for copies in current:
            for cp in copies:
                cp.wait_recv()
            waits += copies
    cores = []
    for part in range(3):
        start, width, _ = PARTS[part]
        src = region("xyz", start, width)
        cp = pltpu.make_async_remote_copy(
            src_ref=src, dst_ref=src, send_sem=core_send.at[part], recv_sem=core_recv.at[part],
            device_id=partner, device_id_type=MESH)
        cp.start()
        cores.append(cp)
    for cp in waits:
        cp.wait_send()
    for cp in cores:
        cp.wait()


def gather_weight(w):
    rows, cols = w.shape
    out = pl.pallas_call(
        gather_weight_kernel,
        in_specs=[pl.BlockSpec(memory_space=pl.ANY)],
        out_specs=pl.BlockSpec(memory_space=pl.ANY),
        out_shape=jax.ShapeDtypeStruct((4, 4, 4, 2, rows, cols), w.dtype),
        scratch_shapes=[pltpu.SemaphoreType.DMA, pltpu.SemaphoreType.DMA((27,)), pltpu.SemaphoreType.DMA((27,)),
                        pltpu.SemaphoreType.DMA((3,)), pltpu.SemaphoreType.DMA((3,))],
        compiler_params=pltpu.CompilerParams(collective_id=0, has_side_effects=True),
        name="gather_weight",
    )(w)
    out = out.reshape(4, 2, 2, 4, 2, rows, cols).transpose(0, 1, 3, 2, 4, 5, 6)
    return out.reshape(128 * rows, cols)


def ctx_gather(x_ref, out_ref, own_sem, send, recv, core_send, core_recv):
    dp, ctx = lax.axis_index("dp"), lax.axis_index("ctx")
    chip, core = ctx // 2, ctx % 2
    partner = (dp, chip * 2 + 1 - core)
    own = pltpu.make_async_copy(x_ref, out_ref.at[0], own_sem)
    own.start()
    pushes = []
    for i in range(1, CHIPS):
        cp = pltpu.make_async_remote_copy(
            src_ref=x_ref, dst_ref=out_ref.at[2 * i], send_sem=send.at[i], recv_sem=recv.at[i],
            device_id=(dp, lax.rem(chip + i, CHIPS) * 2 + core), device_id_type=MESH)
        cp.start()
        pushes.append(cp)
    over = []

    def to_partner(i, src):
        slot = lax.rem(2 * i + 1 - 2 * core + NCTX, NCTX)
        cp = pltpu.make_async_remote_copy(
            src_ref=src, dst_ref=out_ref.at[slot], send_sem=core_send.at[i], recv_sem=core_recv.at[i],
            device_id=partner, device_id_type=MESH)
        cp.start()
        over.append(cp)

    to_partner(0, x_ref)
    for i in range(1, CHIPS):
        pushes[i - 1].wait_recv()
        to_partner(i, out_ref.at[2 * i])
    own.wait()
    return pushes, over


def ctx_peers():
    dp, ctx = lax.axis_index("dp"), lax.axis_index("ctx")
    chip, core = ctx // 2, ctx % 2
    return [(dp, lax.rem(chip + i, CHIPS) * 2 + core) for i in range(1, CHIPS)] + [(dp, chip * 2 + 1 - core)]


def gather_ctx_kernel(x_ref, out_ref, own_sem, send, recv, core_send, core_recv):
    meet(ctx_peers())
    pushes, over = ctx_gather(x_ref, out_ref, own_sem, send, recv, core_send, core_recv)
    for cp in pushes:
        cp.wait_send()
    for cp in over:
        cp.wait()


SEMS = [pltpu.SemaphoreType.DMA] + [pltpu.SemaphoreType.DMA((CHIPS,))] * 4


def gather_ctx(x):
    return pl.pallas_call(
        gather_ctx_kernel,
        in_specs=[pl.BlockSpec(memory_space=pl.ANY)],
        out_specs=pl.BlockSpec(memory_space=pl.ANY),
        out_shape=jax.ShapeDtypeStruct((NCTX,) + x.shape, x.dtype),
        scratch_shapes=SEMS,
        compiler_params=pltpu.CompilerParams(collective_id=1, has_side_effects=True),
        name="gather_key_values",
    )(x)


def gather_grad_kernel(x_ref, a_ref, out_ref, b_ref, own_sem, send, recv, core_send, core_recv, own2, a_send, a_recv):
    dp, ctx = lax.axis_index("dp"), lax.axis_index("ctx")
    peers = [(dp, lax.rem(ctx + j, NCTX)) for j in range(1, NCTX)]
    meet(peers)
    keep = pltpu.make_async_copy(a_ref.at[ctx], b_ref.at[0], own2)
    keep.start()
    pushes, over = ctx_gather(x_ref, out_ref, own_sem, send, recv, core_send, core_recv)
    pieces = []
    for j in range(1, NCTX):
        cp = pltpu.make_async_remote_copy(
            src_ref=a_ref.at[lax.rem(ctx + j, NCTX)], dst_ref=b_ref.at[j], send_sem=a_send.at[j], recv_sem=a_recv.at[j],
            device_id=peers[j - 1], device_id_type=MESH)
        cp.start()
        pieces.append(cp)
    for cp in pushes:
        cp.wait_send()
    for cp in over + pieces:
        cp.wait()
    keep.wait()


def gather_grad(x, a):
    return pl.pallas_call(
        gather_grad_kernel,
        in_specs=[pl.BlockSpec(memory_space=pl.ANY)] * 2,
        out_specs=[pl.BlockSpec(memory_space=pl.ANY)] * 2,
        out_shape=[jax.ShapeDtypeStruct((NCTX,) + x.shape, x.dtype), jax.ShapeDtypeStruct(a.shape, a.dtype)],
        scratch_shapes=SEMS + [pltpu.SemaphoreType.DMA] + [pltpu.SemaphoreType.DMA((NCTX,))] * 2,
        compiler_params=pltpu.CompilerParams(collective_id=2, has_side_effects=True),
        name="gather_grad_projected",
    )(x, a)


def reduce_ctx_kernel(g_ref, out_ref, mine, theirs, landed, mine_sem, core_send, core_recv, send, recv):
    dp, ctx = lax.axis_index("dp"), lax.axis_index("ctx")
    chip, core = ctx // 2, ctx % 2
    partner = (dp, chip * 2 + 1 - core)
    meet(ctx_peers())
    order = list(range(1, CHIPS)) + [0]
    loads, swaps = {}, {}
    for i in order:
        other = lax.rem(2 * i + 2 * core - 1 + NCTX, NCTX)
        swaps[i] = pltpu.make_async_remote_copy(
            src_ref=g_ref.at[other], dst_ref=theirs.at[i], send_sem=core_send.at[i], recv_sem=core_recv.at[i],
            device_id=partner, device_id_type=MESH)
        swaps[i].start()
        loads[i] = pltpu.make_async_copy(g_ref.at[2 * i], mine.at[i], mine_sem.at[i])
        loads[i].start()
    pushes = {}
    for i in order:
        loads[i].wait()
        swaps[i].wait_recv()
        total = mine[i].astype(f32) + theirs[i].astype(f32)
        if i == 0:
            out_ref[...] = total
            continue
        mine[i] = total.astype(bf16)
        pushes[i] = pltpu.make_async_remote_copy(
            src_ref=mine.at[i], dst_ref=landed.at[i], send_sem=send.at[i], recv_sem=recv.at[i],
            device_id=(dp, lax.rem(chip + CHIPS - i, CHIPS) * 2 + core), device_id_type=MESH)
        pushes[i].start()
    for i in range(1, CHIPS):
        pushes[i].wait_recv()
        out_ref[...] += landed[i].astype(f32)
    for i in range(1, CHIPS):
        pushes[i].wait_send()
    for i in order:
        swaps[i].wait_send()


def reduce_ctx(g):
    block = g.shape[1:]
    return pl.pallas_call(
        reduce_ctx_kernel,
        in_specs=[pl.BlockSpec(memory_space=pl.ANY)],
        out_specs=pl.BlockSpec(memory_space=pltpu.VMEM),
        out_shape=jax.ShapeDtypeStruct(block, f32),
        scratch_shapes=[pltpu.VMEM((CHIPS,) + block, bf16)] * 3 + [pltpu.SemaphoreType.DMA((CHIPS,))] * 5,
        compiler_params=pltpu.CompilerParams(
            collective_id=3, has_side_effects=True, vmem_limit_bytes=32 * 2**20),
        name="reduce_key_value_grads",
    )(g)


def reduce_dp_kernel(g_ref, out_ref, landed, send, recv):
    dp, ctx = lax.axis_index("dp"), lax.axis_index("ctx")
    peers = [(lax.rem(dp + j, NDP), ctx) for j in range(1, NDP)]
    meet(peers)
    pushes = []
    for j in range(1, NDP):
        cp = pltpu.make_async_remote_copy(
            src_ref=g_ref.at[lax.rem(dp + j, NDP)], dst_ref=landed.at[j], send_sem=send.at[j], recv_sem=recv.at[j],
            device_id=peers[j - 1], device_id_type=MESH)
        cp.start()
        pushes.append(cp)
    total = g_ref[dp]
    for j in range(1, NDP):
        pushes[j - 1].wait_recv()
        total = total + landed[j]
    out_ref[...] = total
    for cp in pushes:
        cp.wait_send()


def reduce_dp(g):
    block = g.shape[1:]
    return pl.pallas_call(
        reduce_dp_kernel,
        in_specs=[pl.BlockSpec(memory_space=pltpu.VMEM)],
        out_specs=pl.BlockSpec(memory_space=pltpu.VMEM),
        out_shape=jax.ShapeDtypeStruct(block, f32),
        scratch_shapes=[pltpu.VMEM((NDP,) + block, f32)] + [pltpu.SemaphoreType.DMA((NDP,))] * 2,
        compiler_params=pltpu.CompilerParams(
            collective_id=4, has_side_effects=True, vmem_limit_bytes=16 * 2**20),
        name="reduce_grad_weight",
    )(g)


def attention_kernel(blocks, heads, chunk, q_ref, do_ref, kv_ref, out_ref, dq_ref, dkv_ref,
                     s_scr, w_scr, kt_scr, vt_scr, dk_acc, dv_acc):
    T = 128
    R = heads * T
    keys = blocks * T
    t = pl.program_id(1)
    c = lax.axis_index("ctx")
    n_chunks = (c * T) // chunk + 1
    scale = DH ** -0.5

    @pl.when(t == 0)
    def _():
        dk_acc[...] = jnp.zeros_like(dk_acc)
        dv_acc[...] = jnp.zeros_like(dv_acc)
        kt_scr[...] = kv_ref[:, :DH].T
        vt_scr[...] = kv_ref[:, DH:].T

    qs = jnp.concatenate([q_ref[:, g*DH:(g+1)*DH] for g in range(heads)], axis=0)
    per = chunk // T

    def scores(i, mask_diag):
        base = pl.multiple_of(i * chunk, chunk)
        k = kv_ref[pl.ds(base, chunk), :DH]
        s = lax.dot_general(k, qs, (((1,), (1,)), ((), ())), preferred_element_type=f32)
        top = None
        for j in range(per):
            part = s[j*T:(j+1)*T]
            if mask_diag and j == 0:
                kk = lax.broadcasted_iota(jnp.int32, (T, R), 0)
                tok = lax.broadcasted_iota(jnp.int32, (T, R), 1) % T
                part = jnp.where(kk <= tok, part, -jnp.inf)
            else:
                part = jnp.where(i * per + j <= c, part, -jnp.inf)
            s_scr[pl.ds(pl.multiple_of(base + j*T, T), T), :] = part
            m = jnp.max(part.reshape(T//8, 8, R), axis=0)
            top = m if top is None else jnp.maximum(top, m)
        return top

    top8 = scores(0, True)
    top8 = lax.fori_loop(1, n_chunks, lambda i, m: jnp.maximum(m, scores(i, False)), top8)
    top = jnp.max(top8, axis=0, keepdims=True)

    def weigh(i, carry):
        acc, tot = carry
        base = pl.multiple_of(i * chunk, chunk)
        s = s_scr[pl.ds(base, chunk), :]
        w = jnp.exp2((s - top) * (scale * LOG2E))
        tot = tot + jnp.sum(w.reshape(chunk//8, 8, R), axis=0)
        wb = w.astype(bf16)
        w_scr[pl.ds(base, chunk), :] = wb
        acc = acc + jnp.dot(vt_scr[:, pl.ds(base, chunk)], wb, preferred_element_type=f32)
        return acc, tot

    acc, tot8 = lax.fori_loop(0, n_chunks, weigh, (jnp.zeros((DH, R), f32), jnp.zeros((8, R), f32)))
    total = jnp.sum(tot8, axis=0, keepdims=True)
    inv = 1.0 / total
    out_t = acc * inv
    out_tb = out_t.astype(bf16).astype(f32)
    do_t = jnp.concatenate([do_ref[:, g*DH:(g+1)*DH].astype(f32).T for g in range(heads)], axis=1)
    dos_t = (do_t * inv).astype(bf16).astype(f32)
    delta = jnp.sum(dos_t * out_tb, axis=0, keepdims=True)
    dos = jnp.concatenate([dos_t[:, g*DH:(g+1)*DH].T for g in range(heads)], axis=0).astype(bf16)
    for g in range(heads):
        out_ref[:, g*DH:(g+1)*DH] = out_tb[:, g*DH:(g+1)*DH].T.astype(bf16)

    def back(i, dq):
        base = pl.multiple_of(i * chunk, chunk)
        v = kv_ref[pl.ds(base, chunk), DH:]
        dp = lax.dot_general(v, dos, (((1,), (1,)), ((), ())), preferred_element_type=f32)
        wb = w_scr[pl.ds(base, chunk), :]
        ds = (dp - delta).astype(bf16) * wb
        dq = dq + jnp.dot(kt_scr[:, pl.ds(base, chunk)], ds, preferred_element_type=f32)
        dk_acc[pl.ds(base, chunk), :] += jnp.dot(ds, qs, preferred_element_type=f32)
        dv_acc[pl.ds(base, chunk), :] += jnp.dot(wb, dos, preferred_element_type=f32)
        return dq

    dq = lax.fori_loop(0, n_chunks, back, jnp.zeros((DH, R), f32)) * scale
    for g in range(heads):
        dq_ref[:, g*DH:(g+1)*DH] = dq[:, g*DH:(g+1)*DH].T.astype(bf16)

    @pl.when(t == pl.num_programs(1) - 1)
    def _():
        dkv_ref[:, :DH] = (dk_acc[...] * scale).astype(bf16)
        dkv_ref[:, DH:] = dv_acc[...].astype(bf16)


def attention(q, do, kv, heads=4, chunk=1024):
    T, HD = q.shape
    keys, width = kv.shape
    kvh = width // (2*DH)
    R = heads*T
    tiles = HD // DH // kvh // heads
    return pl.pallas_call(
        functools.partial(attention_kernel, keys//T, heads, chunk),
        grid=(kvh, tiles),
        in_specs=[pl.BlockSpec((T, heads*DH), lambda h, t: (0, h*tiles+t)),
                  pl.BlockSpec((T, heads*DH), lambda h, t: (0, h*tiles+t)),
                  pl.BlockSpec((keys, 2*DH), lambda h, t: (0, h))],
        out_specs=[pl.BlockSpec((T, heads*DH), lambda h, t: (0, h*tiles+t)),
                   pl.BlockSpec((T, heads*DH), lambda h, t: (0, h*tiles+t)),
                   pl.BlockSpec((keys, 2*DH), lambda h, t: (0, h))],
        out_shape=[jax.ShapeDtypeStruct(q.shape, jnp.bfloat16)]*2 + [jax.ShapeDtypeStruct(kv.shape, jnp.bfloat16)],
        scratch_shapes=[pltpu.VMEM((keys, R), jnp.float32), pltpu.VMEM((keys, R), jnp.bfloat16),
                        pltpu.VMEM((DH, keys), jnp.bfloat16), pltpu.VMEM((DH, keys), jnp.bfloat16),
                        pltpu.VMEM((keys, DH), jnp.float32), pltpu.VMEM((keys, DH), jnp.float32)],
        compiler_params=pltpu.CompilerParams(vmem_limit_bytes=48*2**20),
        name="attention",
    )(q, do, kv)


def on_device(inputs, queries, grad_output, kv_weight):
    tokens = inputs[0]
    count, features = tokens.shape
    width = kv_weight.shape[1]
    half = width // 2
    heads = half // DH
    ctx = lax.axis_index("ctx")
    tables = rope_tables(ctx * count + jnp.arange(count, dtype=jnp.int32), DH)

    weight = gather_weight(kv_weight)
    projected = jnp.dot(tokens, weight, preferred_element_type=f32)
    keys = rotary(projected[:, :half].reshape(count, heads, DH), tables, 1.0).astype(bf16)
    values = projected[:, half:].reshape(count, heads, DH).astype(bf16)
    own = jnp.concatenate([keys, values], axis=-1).reshape(count, width)
    kv = gather_ctx(own).reshape(NCTX * count, width)

    attn_out, grad_query, terms = attention(queries[0], grad_output[0], kv)

    grads = reduce_ctx(terms.reshape(NCTX, count, width)).reshape(count, heads, 2 * DH)
    grad_keys = rotary(grads[..., :DH], tables, -1.0).reshape(count, half)
    grad_values = grads[..., DH:].reshape(count, half)
    grad_projected = jnp.concatenate([grad_keys, grad_values], axis=1).astype(bf16)

    pieces = tokens.reshape(count, NDP, NCTX, -1).transpose(2, 0, 1, 3).reshape(NCTX, count, features // NCTX)
    all_grads, all_tokens = gather_grad(grad_projected, pieces)
    grad_inputs = lax.dot_general(
        grad_projected, weight, (((1,), (1,)), ((), ())), preferred_element_type=f32
    ).astype(bf16)
    part = lax.dot_general(
        all_tokens.reshape(NCTX * count, -1), all_grads.reshape(NCTX * count, width),
        (((0,), (0,)), ((), ())), preferred_element_type=f32)
    grad_weight = reduce_dp(part.reshape(NDP, -1, width))
    return (attn_out[None], grad_query[None], grad_inputs[None], grad_weight)


def solution(mesh):
    tokens = P("dp", "ctx", None)
    rows = P(("dp", "ctx"), None)
    return jax.shard_map(
        on_device, mesh=mesh, in_specs=(tokens, tokens, tokens, rows),
        out_specs=(tokens, tokens, tokens, rows), check_vma=False)
```

```python
import functools
import math

import jax
import jax.numpy as jnp
from jax import lax
from jax.experimental import pallas as pl
from jax.experimental.pallas import tpu as pltpu
from jax.sharding import PartitionSpec as P

DH = 128
LOG2E = math.log2(math.e)
ROPE_BASE = 500000.0
MESH = pl.DeviceIdType.MESH
NDP, NCTX = 8, 16
CHIPS = NCTX // 2
f32, bf16 = jnp.float32, jnp.bfloat16


def rope_tables(positions, head_dim):
    half_dim = head_dim // 2
    frequency = ROPE_BASE ** (-2.0 * jnp.arange(half_dim, dtype=f32) / head_dim)
    angles = positions.astype(f32)[:, None] * frequency[None, :]
    return (jnp.cos(angles)[:, None, :], jnp.sin(angles)[:, None, :])


def rotary(values, tables, sign):
    half_dim = values.shape[-1] // 2
    cosine, sine = tables
    a = values[..., :half_dim]
    b = values[..., half_dim:]
    return jnp.concatenate([a * cosine - sign * b * sine, b * cosine + sign * a * sine], axis=-1)


def position():
    dp, ctx = lax.axis_index("dp"), lax.axis_index("ctx")
    return dp // 2, dp % 2, ctx // 4, (ctx // 2) % 2, ctx % 2


def device_at(y, zh, x, zl, core):
    return (y * 2 + zh, x * 4 + zl * 2 + core)


def meet(peers):
    barrier = pltpu.get_barrier_semaphore()
    for peer in peers:
        pl.semaphore_signal(barrier, inc=1, device_id=peer, device_id_type=MESH)
    pl.semaphore_wait(barrier, len(peers))


PARTS = ((0, 384, "zyx"), (384, 384, "yxz"), (768, 256, "xzy"))


def gather_weight_kernel(w_ref, out_ref, own_sem, send, recv, core_send, core_recv):
    y, zh, x, zl, core = position()
    z = zh * 2 + zl

    def peer(axis, step):
        if axis == "x":
            return device_at(y, zh, lax.rem(x + step, 4), zl, core)
        if axis == "y":
            return device_at(lax.rem(y + step, 4), zh, x, zl, core)
        far = lax.rem(z + step, 4)
        return device_at(y, far // 2, x, lax.rem(far, 2), core)

    partner = device_at(y, zh, x, zl, 1 - core)
    meet([peer(axis, step) for axis in "xyz" for step in (1, 2, 3)] + [partner])

    def region(done, start, width):
        yy = slice(None) if "y" in done else y
        xx = slice(None) if "x" in done else x
        zh_, zl_ = (slice(None), slice(None)) if "z" in done else (zh, zl)
        return out_ref.at[yy, zh_, xx, zl_, core, :, pl.ds(start, width)]

    own = pltpu.make_async_copy(w_ref, out_ref.at[y, zh, x, zl, core], own_sem)
    own.start()
    own.wait()
    waits = []

    def push(part, phase):
        start, width, order = PARTS[part]
        src = region(order[:phase], start, width)
        copies = []
        for step in (1, 2, 3):
            k = (part * 3 + phase) * 3 + step - 1
            cp = pltpu.make_async_remote_copy(
                src_ref=src, dst_ref=src, send_sem=send.at[k], recv_sem=recv.at[k],
                device_id=peer(order[phase], step), device_id_type=MESH)
            cp.start()
            copies.append(cp)
        return copies

    for phase in range(3):
        current = [push(part, phase) for part in range(3)]
        for copies in current:
            for cp in copies:
                cp.wait_recv()
            waits += copies
    cores = []
    for part in range(3):
        start, width, _ = PARTS[part]
        src = region("xyz", start, width)
        cp = pltpu.make_async_remote_copy(
            src_ref=src, dst_ref=src, send_sem=core_send.at[part], recv_sem=core_recv.at[part],
            device_id=partner, device_id_type=MESH)
        cp.start()
        cores.append(cp)
    for cp in waits:
        cp.wait_send()
    for cp in cores:
        cp.wait()


def gather_weight(w):
    rows, cols = w.shape
    out = pl.pallas_call(
        gather_weight_kernel,
        in_specs=[pl.BlockSpec(memory_space=pl.ANY)],
        out_specs=pl.BlockSpec(memory_space=pl.ANY),
        out_shape=jax.ShapeDtypeStruct((4, 2, 4, 2, 2, rows, cols), w.dtype),
        scratch_shapes=[pltpu.SemaphoreType.DMA, pltpu.SemaphoreType.DMA((27,)), pltpu.SemaphoreType.DMA((27,)),
                        pltpu.SemaphoreType.DMA((3,)), pltpu.SemaphoreType.DMA((3,))],
        compiler_params=pltpu.CompilerParams(collective_id=0, has_side_effects=True),
        name="gather_weight",
    )(w)
    return out.reshape(128 * rows, cols)


QHEADS = 4
KVH = 4
T = 128


def main_kernel(tiles, q_ref, do_ref, own_ref, tok_ref, w_hbm, cos_ref, sin_ref,
                out_ref, dq_ref, gin_ref, gw_ref,
                kv, s_scr, wt_scr, kt_scr, vt_scr, dk_acc, dv_acc,
                even, odd, theirs, landed, own32, gp_all, gp_own, weight, tok_all, tok_t, dw, dw_landed,
                local, kv_send, kv_recv, fw_send, fw_recv, swap_send, swap_recv, ps_send, ps_recv,
                ag_send, ag_recv, agf_send, agf_recv, dw_send, dw_recv, a_send, a_recv):
    dp, c = lax.axis_index("dp"), lax.axis_index("ctx")
    chip, core = c // 2, c % 2
    partner = (dp, chip * 2 + 1 - core)
    h, t = pl.program_id(0), pl.program_id(1)
    R = QHEADS * T
    keys = NCTX * T
    scale = DH ** -0.5
    far = list(range(1, CHIPS))

    def chip_at(i):
        return (dp, lax.rem(chip + i + CHIPS, CHIPS) * 2 + core)

    def remote(src, dst, send, recv, device):
        return pltpu.make_async_remote_copy(
            src_ref=src, dst_ref=dst, send_sem=send, recv_sem=recv, device_id=device, device_id_type=MESH)

    def kv_push(hd, i):
        return remote(own_ref.at[hd], kv.at[hd, 2 * i], kv_send.at[hd, i], kv_recv.at[hd, i], chip_at(i))

    def kv_own(hd):
        return remote(own_ref.at[hd], kv.at[hd, 1], fw_send.at[hd, 0], fw_recv.at[hd, 0], partner)

    def kv_forward(hd, i):
        return remote(kv.at[hd, 2 * i], kv.at[hd, 2 * i + 1 - 2 * core], fw_send.at[hd, i], fw_recv.at[hd, i], partner)

    def swap(hd):
        return remote(odd.at[hd], theirs.at[hd], swap_send.at[hd], swap_recv.at[hd], partner)

    def sum_push(hd, i):
        return remote(even.at[hd, i], landed.at[hd, i], ps_send.at[hd, i], ps_recv.at[hd, i], chip_at(-i))

    def gp_push(hd, i):
        return remote(gp_all.at[hd, 0], gp_all.at[hd, 2 * i], ag_send.at[hd, i], ag_recv.at[hd, i], chip_at(i))

    def gp_forward(hd, i):
        slot = lax.rem(2 * i + 1 - 2 * core + NCTX, NCTX)
        return remote(gp_all.at[hd, 2 * i], gp_all.at[hd, slot], agf_send.at[hd, i], agf_recv.at[hd, i], partner)

    def tok_push(j):
        to = lax.rem(c + j, NCTX)
        return remote(tok_ref.at[to], tok_all.at[j], a_send.at[j], a_recv.at[j], (dp, to))

    def dw_push(hd, j):
        to = lax.rem(dp + j, NDP)
        return remote(dw.at[hd, to], dw_landed.at[hd, j], dw_send.at[hd, j], dw_recv.at[hd, j], (to, c))

    own_copy = pltpu.make_async_copy(own_ref, kv.at[:, 0], local.at[0])
    weight_copy = pltpu.make_async_copy(w_hbm, weight, local.at[1])
    tok_copy = pltpu.make_async_copy(tok_ref.at[c], tok_all.at[0], local.at[2])

    def forward_keys(hd):
        for i in far:
            @pl.when(i <= chip)
            def _():
                kv_push(hd, i).wait_recv()
                kv_forward(hd, i).start()

    def await_keys(hd):
        for i in far:
            @pl.when(i <= chip)
            def _():
                kv_forward(hd, i).wait_recv()

        @pl.when(core == 1)
        def _():
            kv_own(hd).wait_recv()

    def add_pair(hd):
        swap(hd).wait_recv()
        own32[...] = even[hd, 0].astype(f32) + theirs[hd, lax.rem(CHIPS - core, CHIPS)].astype(f32)
        for i in far:
            @pl.when(i <= chip)
            def _():
                total = even[hd, i].astype(f32) + theirs[hd, i - core].astype(f32)
                even[hd, i] = total.astype(bf16)
                sum_push(hd, i).start()

    def finish_block(hd):
        for i in far:
            @pl.when(chip + i < CHIPS)
            def _():
                sum_push(hd, i).wait_recv()
                own32[...] += landed[hd, i].astype(f32)
        key_part = own32[:, :DH]
        key_part = (key_part * cos_ref[...] + pltpu.roll(key_part, DH // 2, 1) * sin_ref[...]).astype(bf16)
        value_part = own32[:, DH:].astype(bf16)
        gp_all[hd, 0, :, :DH] = key_part
        gp_all[hd, 0, :, DH:] = value_part
        gp_own[hd] = key_part
        gp_own[KVH + hd] = value_part
        for i in far:
            gp_push(hd, i).start()
        gp_forward(hd, 0).start()

    def forward_grads(hd):
        for i in far:
            gp_push(hd, i).wait_recv()
            gp_forward(hd, i).start()

    def weight_grad(hd):
        for i in range(CHIPS):
            gp_forward(hd, i).wait_recv()
        part = jnp.dot(tok_t[...], gp_all[hd].reshape(keys, 2 * DH), preferred_element_type=f32)
        dw[hd] = part.reshape(dw.shape[1:])
        for j in range(1, NDP):
            dw_push(hd, j).start()

    @pl.when((h == 0) & (t == 0))
    def _():
        meet([(dp, lax.rem(c + j, NCTX)) for j in range(1, NCTX)]
             + [(lax.rem(dp + j, NDP), c) for j in range(1, NDP)])
        own_copy.start()
        for hd in range(KVH):
            for i in far:
                @pl.when(chip + i < CHIPS)
                def _():
                    kv_push(hd, i).start()

            @pl.when(core == 0)
            def _():
                kv_own(hd).start()
        weight_copy.start()
        tok_copy.start()
        for j in range(1, NCTX):
            tok_push(j).start()
        for j in range(1, NCTX):
            @pl.when(j > c)
            def _():
                kv[:, j] = jnp.zeros((KVH, T, 2 * DH), bf16)
        own_copy.wait()
        forward_keys(0)

    @pl.when(t == 0)
    def _():
        await_keys(h)
        dk_acc[...] = jnp.zeros_like(dk_acc)
        dv_acc[...] = jnp.zeros_like(dv_acc)
        kt_scr[...] = kv[h, :, :, :DH].reshape(keys, DH).T
        vt_scr[...] = kv[h, :, :, DH:].reshape(keys, DH).T

    qs = jnp.concatenate([q_ref[:, g*DH:(g+1)*DH] for g in range(QHEADS)], axis=0)
    k = kv[h, :, :, :DH].reshape(keys, DH)
    v = kv[h, :, :, DH:].reshape(keys, DH)
    s = lax.dot_general(k, qs, (((1,), (1,)), ((), ())), preferred_element_type=f32)
    top = None
    for j in range(NCTX):
        part = s[j*T:(j+1)*T]
        if j == 0:
            key = lax.broadcasted_iota(jnp.int32, (T, R), 0)
            token = lax.broadcasted_iota(jnp.int32, (T, R), 1) % T
            part = jnp.where(key <= token, part, -jnp.inf)
        else:
            part = jnp.where(j <= c, part, -jnp.inf)
        s_scr[pl.ds(j*T, T), :] = part
        best = jnp.max(part.reshape(T//8, 8, R), axis=0)
        top = best if top is None else jnp.maximum(top, best)
    top = jnp.max(top, axis=0, keepdims=True)

    weights = jnp.exp2((s_scr[...] - top) * (scale * LOG2E))
    total = jnp.sum(jnp.sum(weights.reshape(keys//8, 8, R), axis=0), axis=0, keepdims=True)
    wt_scr[...] = weights.astype(bf16)
    acc = jnp.dot(vt_scr[...], wt_scr[...], preferred_element_type=f32)
    inv = 1.0 / total
    out_t = (acc * inv).astype(bf16).astype(f32)
    do_t = jnp.concatenate([do_ref[:, g*DH:(g+1)*DH].astype(f32).T for g in range(QHEADS)], axis=1)
    dos_t = (do_t * inv).astype(bf16).astype(f32)
    delta = jnp.sum(dos_t * out_t, axis=0, keepdims=True)
    dos = jnp.concatenate([dos_t[:, g*DH:(g+1)*DH].T for g in range(QHEADS)], axis=0).astype(bf16)
    for g in range(QHEADS):
        out_ref[:, g*DH:(g+1)*DH] = out_t[:, g*DH:(g+1)*DH].T.astype(bf16)

    dprobs = lax.dot_general(v, dos, (((1,), (1,)), ((), ())), preferred_element_type=f32)
    wb = wt_scr[...]
    ds = (dprobs - delta).astype(bf16) * wb
    dq = jnp.dot(kt_scr[...], ds, preferred_element_type=f32) * scale
    dk_acc[...] += jnp.dot(ds, qs, preferred_element_type=f32)
    dv_acc[...] += jnp.dot(wb, dos, preferred_element_type=f32)
    for g in range(QHEADS):
        dq_ref[:, g*DH:(g+1)*DH] = dq[:, g*DH:(g+1)*DH].T.astype(bf16)

    @pl.when((t == 0) & (h >= 1))
    def _():
        add_pair(h - 1)

    @pl.when((t == 0) & (h >= 2))
    def _():
        forward_grads(h - 2)

    @pl.when((t == 1) & (h < KVH - 1))
    def _():
        forward_keys(h + 1)

    @pl.when((t == 1) & (h == 1))
    def _():
        tok_copy.wait()
        for j in range(1, NCTX):
            tok_push(j).wait_recv()
        tok_t[...] = tok_all[...].reshape(keys, -1).T

    @pl.when((t == 2) & (h >= 1))
    def _():
        finish_block(h - 1)

    @pl.when((t == 2) & (h >= 2))
    def _():
        weight_grad(h - 2)

    @pl.when(t == tiles - 1)
    def _():
        for q in range(CHIPS):
            for parity, ref in ((0, even), (1, odd)):
                rows = pl.ds((2 * q + parity) * T, T)
                ref[h, q, :, :DH] = (dk_acc[rows, :] * scale).astype(bf16)
                ref[h, q, :, DH:] = dv_acc[rows, :].astype(bf16)
        swap(h).start()

    @pl.when((t == tiles - 1) & (h == KVH - 1))
    def _():
        last = KVH - 1
        forward_grads(last - 1)
        add_pair(last)
        weight_grad(last - 1)
        finish_block(last)
        weight_copy.wait()
        gp = jnp.concatenate([gp_own[n] for n in range(2 * KVH)], axis=1)
        block = 512

        def inputs_part(n, carry):
            rows = pl.ds(pl.multiple_of(n * block, block), block)
            gin_ref[:, rows] = lax.dot_general(
                gp, weight[rows, :], (((1,), (1,)), ((), ())), preferred_element_type=f32).astype(bf16)
            return carry

        lax.fori_loop(0, weight.shape[0] // block, inputs_part, 0)
        forward_grads(last)
        weight_grad(last)
        for hd in range(KVH):
            total_w = dw[hd, dp]
            for j in range(1, NDP):
                dw_push(hd, j).wait_recv()
                total_w = total_w + dw_landed[hd, j]
            gw_ref[:, hd*DH:(hd+1)*DH] = total_w[:, :DH]
            gw_ref[:, (KVH+hd)*DH:(KVH+hd+1)*DH] = total_w[:, DH:]
        for hd in range(KVH):
            for i in far:
                @pl.when(chip + i < CHIPS)
                def _():
                    kv_push(hd, i).wait_send()

                @pl.when(i <= chip)
                def _():
                    kv_forward(hd, i).wait_send()
                    sum_push(hd, i).wait_send()

                gp_push(hd, i).wait_send()

            @pl.when(core == 0)
            def _():
                kv_own(hd).wait_send()

            swap(hd).wait_send()
            for i in range(CHIPS):
                gp_forward(hd, i).wait_send()
            for j in range(1, NDP):
                dw_push(hd, j).wait_send()
        for j in range(1, NCTX):
            tok_push(j).wait_send()


def main(q, do, own, pieces, weight, cosine, sine):
    tiles = q.shape[1] // DH // KVH // QHEADS
    keys, R = NCTX * T, QHEADS * T
    tile = pl.BlockSpec((T, R), lambda h, t: (0, h * tiles + t))
    hbm = pl.BlockSpec(memory_space=pl.ANY)
    table = pl.BlockSpec((T, DH), lambda h, t: (0, 0))
    features, width = weight.shape
    per = features // NCTX
    rows = per // NDP
    dma = pltpu.SemaphoreType.DMA
    return pl.pallas_call(
        functools.partial(main_kernel, tiles),
        grid=(KVH, tiles),
        in_specs=[tile, tile, hbm, hbm, hbm, table, table],
        out_specs=[tile, tile,
                   pl.BlockSpec((T, features), lambda h, t: (0, 0)),
                   pl.BlockSpec((rows, width), lambda h, t: (0, 0))],
        out_shape=[jax.ShapeDtypeStruct(q.shape, bf16), jax.ShapeDtypeStruct(q.shape, bf16),
                   jax.ShapeDtypeStruct((T, features), bf16), jax.ShapeDtypeStruct((rows, width), f32)],
        scratch_shapes=[
            pltpu.VMEM((KVH, NCTX, T, 2 * DH), bf16),
            pltpu.VMEM((keys, R), f32), pltpu.VMEM((keys, R), bf16),
            pltpu.VMEM((DH, keys), bf16), pltpu.VMEM((DH, keys), bf16),
            pltpu.VMEM((keys, DH), f32), pltpu.VMEM((keys, DH), f32),
            pltpu.VMEM((KVH, CHIPS, T, 2 * DH), bf16),
            pltpu.VMEM((KVH, CHIPS, T, 2 * DH), bf16),
            pltpu.VMEM((KVH, CHIPS, T, 2 * DH), bf16),
            pltpu.VMEM((KVH, CHIPS, T, 2 * DH), bf16),
            pltpu.VMEM((T, 2 * DH), f32),
            pltpu.VMEM((KVH, NCTX, T, 2 * DH), bf16),
            pltpu.VMEM((2 * KVH, T, DH), bf16),
            pltpu.VMEM((features, width), bf16),
            pltpu.VMEM((NCTX, T, per), bf16), pltpu.VMEM((per, keys), bf16),
            pltpu.VMEM((KVH, NDP, rows, 2 * DH), f32), pltpu.VMEM((KVH, NDP, rows, 2 * DH), f32),
            dma((3,)), dma((KVH, CHIPS)), dma((KVH, CHIPS)), dma((KVH, CHIPS)), dma((KVH, CHIPS)),
            dma((KVH,)), dma((KVH,)), dma((KVH, CHIPS)), dma((KVH, CHIPS)),
            dma((KVH, CHIPS)), dma((KVH, CHIPS)), dma((KVH, CHIPS)), dma((KVH, CHIPS)),
            dma((KVH, NDP)), dma((KVH, NDP)), dma((NCTX,)), dma((NCTX,))],
        compiler_params=pltpu.CompilerParams(
            collective_id=1, has_side_effects=True, vmem_limit_bytes=58 * 2**20),
        name="attention_and_exchanges",
    )(q, do, own, pieces, weight, cosine, sine)


def on_device(inputs, queries, grad_output, kv_weight):
    tokens = inputs[0]
    count, features = tokens.shape
    half = kv_weight.shape[1] // 2
    heads = half // DH
    ctx = lax.axis_index("ctx")
    cosine, sine = rope_tables(ctx * count + jnp.arange(count, dtype=jnp.int32), DH)

    weight = gather_weight(kv_weight)
    projected = jnp.dot(tokens, weight, preferred_element_type=f32)
    keys = rotary(projected[:, :half].reshape(count, heads, DH), (cosine, sine), 1.0).astype(bf16)
    values = projected[:, half:].reshape(count, heads, DH).astype(bf16)
    own = jnp.concatenate([keys, values], axis=-1).transpose(1, 0, 2)
    pieces = tokens.reshape(count, NDP, NCTX, -1).transpose(2, 0, 1, 3).reshape(NCTX, count, features // NCTX)
    cosine, sine = cosine[:, 0], sine[:, 0]
    attn_out, grad_query, grad_inputs, grad_weight = main(
        queries[0], grad_output[0], own, pieces, weight,
        jnp.concatenate([cosine, cosine], axis=1), jnp.concatenate([sine, -sine], axis=1))
    return (attn_out[None], grad_query[None], grad_inputs[None], grad_weight)


def solution(mesh):
    tokens = P("dp", "ctx", None)
    rows = P(("dp", "ctx"), None)
    return jax.shard_map(
        on_device, mesh=mesh, in_specs=(tokens, tokens, tokens, rows),
        out_specs=(tokens, tokens, tokens, rows), check_vma=False)
```

```python
import functools
import math

import jax
import jax.numpy as jnp
from jax import lax
from jax.experimental import pallas as pl
from jax.experimental.pallas import tpu as pltpu
from jax.sharding import PartitionSpec as P

DH = 128
LOG2E = math.log2(math.e)
ROPE_BASE = 500000.0
MESH = pl.DeviceIdType.MESH
NDP, NCTX = 8, 16
CHIPS = NCTX // 2
f32, bf16 = jnp.float32, jnp.bfloat16


def rope_tables(positions, head_dim):
    half_dim = head_dim // 2
    frequency = ROPE_BASE ** (-2.0 * jnp.arange(half_dim, dtype=f32) / head_dim)
    angles = positions.astype(f32)[:, None] * frequency[None, :]
    return jnp.cos(angles), jnp.sin(angles)


def position():
    dp, ctx = lax.axis_index("dp"), lax.axis_index("ctx")
    return dp // 2, dp % 2, ctx // 4, (ctx // 2) % 2, ctx % 2


def device_at(y, zh, x, zl, core):
    return (y * 2 + zh, x * 4 + zl * 2 + core)


def meet(peers):
    barrier = pltpu.get_barrier_semaphore()
    for peer in peers:
        pl.semaphore_signal(barrier, inc=1, device_id=peer, device_id_type=MESH)
    pl.semaphore_wait(barrier, len(peers))


QHEADS = 4
KVH = 4
T = 128


def main_kernel(tiles, q_ref, do_ref, tok_ref, w_ref, cos_ref, sin_ref,
                out_ref, dq_ref, gin_ref, gw_ref,
                kv, s_scr, wt_scr, kt_scr, vt_scr, dk_acc, dv_acc,
                even, odd, theirs, landed, own32, gp_all, gp_own, weight, tok_own, tok_t, dw, dw_landed,
                w_send, w_recv, ws_send, ws_recv, tok_local, kv_send, kv_recv, fw_send, fw_recv, swap_send, swap_recv, ps_send, ps_recv,
                ag_send, ag_recv, agf_send, agf_recv, dw_send, dw_recv, a_send, a_recv):
    dp, c = lax.axis_index("dp"), lax.axis_index("ctx")
    chip, core = c // 2, c % 2
    partner = (dp, chip * 2 + 1 - core)
    h, t = pl.program_id(0), pl.program_id(1)
    R = QHEADS * T
    keys = NCTX * T
    scale = DH ** -0.5
    far = list(range(1, CHIPS))
    y, zh, x, zl, _ = position()
    z = zh * 2 + zl

    def chip_at(i):
        return (dp, lax.rem(chip + i + CHIPS, CHIPS) * 2 + core)

    def remote(src, dst, send, recv, device):
        return pltpu.make_async_remote_copy(
            src_ref=src, dst_ref=dst, send_sem=send, recv_sem=recv, device_id=device, device_id_type=MESH)

    def w_axes(hd, u):
        return ("zyx", "yxz", "xzy")[(2 * hd + u) % 3]

    def along(axis, step):
        if axis == "x":
            return device_at(y, zh, lax.rem(x + step, 4), zl, core)
        if axis == "y":
            return device_at(lax.rem(y + step, 4), zh, x, zl, core)
        to = lax.rem(z + step, 4)
        return device_at(y, to // 2, x, lax.rem(to, 2), core)

    def w_region(hd, u, done):
        yy = slice(None) if "y" in done else y
        xx = slice(None) if "x" in done else x
        zz, zzl = (slice(None), slice(None)) if "z" in done else (zh, zl)
        return weight.at[hd, u, yy, zz, xx, zzl, core]

    def w_push(hd, u, phase, step):
        axes = w_axes(hd, u)
        region = w_region(hd, u, axes[:phase])
        n = ((hd * 2 + u) * 3 + phase) * 3 + step - 1
        return remote(region, region, w_send.at[n], w_recv.at[n], along(axes[phase], step))

    def w_start(hd, phase):
        for u in range(2):
            for step in (1, 2, 3):
                w_push(hd, u, phase, step).start()

    def w_arrived(hd, phase):
        for u in range(2):
            for step in (1, 2, 3):
                w_push(hd, u, phase, step).wait_recv()

    def w_swap(hd, u):
        region = w_region(hd, u, "xyz")
        return remote(region, region, ws_send.at[hd, u], ws_recv.at[hd, u], partner)

    def w_share(hd):
        for u in range(2):
            for step in (1, 2, 3):
                w_push(hd, u, 2, step).wait_recv()
            w_swap(hd, u).start()

    def project(hd):
        for u in range(2):
            w_swap(hd, u).wait_recv()
        features = tok_ref.shape[1]
        key_part = jnp.dot(tok_ref[...], weight[hd, 0].reshape(features, DH), preferred_element_type=f32)
        kv[hd, 0, :, :DH] = (key_part * cos_ref[...] - pltpu.roll(key_part, DH // 2, 1) * sin_ref[...]).astype(bf16)
        kv[hd, 0, :, DH:] = jnp.dot(
            tok_ref[...], weight[hd, 1].reshape(features, DH), preferred_element_type=f32).astype(bf16)
        for i in far:
            @pl.when(chip + i < CHIPS)
            def _():
                kv_push(hd, i).start()

        @pl.when(core == 0)
        def _():
            kv_own(hd).start()

    def kv_push(hd, i):
        return remote(kv.at[hd, 0], kv.at[hd, 2 * i], kv_send.at[hd, i], kv_recv.at[hd, i], chip_at(i))

    def kv_own(hd):
        return remote(kv.at[hd, 0], kv.at[hd, 1], fw_send.at[hd, 0], fw_recv.at[hd, 0], partner)

    def kv_forward(hd, i):
        return remote(kv.at[hd, 2 * i], kv.at[hd, 2 * i + 1 - 2 * core], fw_send.at[hd, i], fw_recv.at[hd, i], partner)

    def swap(hd):
        return remote(odd.at[hd], theirs.at[hd], swap_send.at[hd], swap_recv.at[hd], partner)

    def sum_push(hd, i):
        return remote(even.at[hd, i], landed.at[hd, i], ps_send.at[hd, i], ps_recv.at[hd, i], chip_at(-i))

    def gp_push(hd, i):
        return remote(gp_all.at[hd, 0], gp_all.at[hd, 2 * i], ag_send.at[hd, i], ag_recv.at[hd, i], chip_at(i))

    def gp_forward(hd, i):
        slot = lax.rem(2 * i + 1 - 2 * core + NCTX, NCTX)
        return remote(gp_all.at[hd, 2 * i], gp_all.at[hd, slot], agf_send.at[hd, i], agf_recv.at[hd, i], partner)

    def tok_push(j):
        to = lax.rem(c + j, NCTX)
        return remote(tok_own.at[:, to], tok_t.at[:, :, pl.ds(j * T, T)], a_send.at[j], a_recv.at[j], (dp, to))

    def dw_push(hd, j):
        to = lax.rem(dp + j, NDP)
        return remote(dw.at[hd, to], dw_landed.at[hd, j], dw_send.at[hd, j], dw_recv.at[hd, j], (to, c))

    tok_copy = pltpu.make_async_copy(tok_own.at[:, c], tok_t.at[:, :, pl.ds(0, T)], tok_local)

    def forward_keys(hd):
        for i in far:
            @pl.when(i <= chip)
            def _():
                kv_push(hd, i).wait_recv()
                kv_forward(hd, i).start()

    def await_keys(hd):
        for i in far:
            @pl.when(i <= chip)
            def _():
                kv_forward(hd, i).wait_recv()

        @pl.when(core == 1)
        def _():
            kv_own(hd).wait_recv()

    def add_pair(hd):
        swap(hd).wait_recv()
        own32[...] = even[hd, 0].astype(f32) + theirs[hd, lax.rem(CHIPS - core, CHIPS)].astype(f32)
        for i in far:
            @pl.when(i <= chip)
            def _():
                total = even[hd, i].astype(f32) + theirs[hd, i - core].astype(f32)
                even[hd, i] = total.astype(bf16)
                sum_push(hd, i).start()

    def finish_block(hd):
        for i in far:
            @pl.when(chip + i < CHIPS)
            def _():
                sum_push(hd, i).wait_recv()
                own32[...] += landed[hd, i].astype(f32)
        key_part = own32[:, :DH]
        key_part = (key_part * cos_ref[...] + pltpu.roll(key_part, DH // 2, 1) * sin_ref[...]).astype(bf16)
        value_part = own32[:, DH:].astype(bf16)
        gp_all[hd, 0, :, :DH] = key_part
        gp_all[hd, 0, :, DH:] = value_part
        gp_own[2 * hd] = key_part
        gp_own[2 * hd + 1] = value_part
        for i in far:
            gp_push(hd, i).start()
        gp_forward(hd, 0).start()

    def forward_grads(hd):
        for i in far:
            gp_push(hd, i).wait_recv()
            gp_forward(hd, i).start()

    def weight_grad(hd):
        for i in range(CHIPS):
            gp_forward(hd, i).wait_recv()
        part = jnp.dot(tok_t[...].reshape(-1, keys), gp_all[hd].reshape(keys, 2 * DH), preferred_element_type=f32)
        dw[hd] = part.reshape(dw.shape[1:])
        for j in range(1, NDP):
            dw_push(hd, j).start()

    @pl.when((h == 0) & (t == 0))
    def _():
        meet([(dp, lax.rem(c + j, NCTX)) for j in range(1, NCTX)]
             + [(lax.rem(dp + j, NDP), c) for j in range(1, NDP)]
             + [along(axis, k) for axis in "xyz" for k in (1, 2, 3)])
        for hd in range(KVH):
            for u in range(2):
                first = (u * KVH + hd) * DH
                weight[hd, u, y, zh, x, zl, core] = w_ref[:, first:first + DH]
        for hd in range(KVH):
            w_start(hd, 0)
        w_arrived(0, 0)
        w_start(0, 1)
        rows = tok_own.shape[2]
        for n in range(tok_ref.shape[1] // T):
            turned = tok_ref[:, n*T:(n+1)*T].T
            for m in range(T // rows):
                g = n * (T // rows) + m
                tok_own[g // NCTX, g % NCTX] = turned[m*rows:(m+1)*rows]
        for j in range(1, NCTX):
            @pl.when(j > c)
            def _():
                kv[:, j] = jnp.zeros((KVH, T, 2 * DH), bf16)
        w_arrived(0, 1)
        w_start(0, 2)
        for hd in range(1, KVH):
            w_arrived(hd, 0)
            w_start(hd, 1)
        w_share(0)
        project(0)
        w_arrived(1, 1)
        w_start(1, 2)
        forward_keys(0)

    @pl.when(t == 0)
    def _():
        await_keys(h)
        dk_acc[...] = jnp.zeros_like(dk_acc)
        dv_acc[...] = jnp.zeros_like(dv_acc)
        kt_scr[...] = kv[h, :, :, :DH].reshape(keys, DH).T
        vt_scr[...] = kv[h, :, :, DH:].reshape(keys, DH).T

    qs = jnp.concatenate([q_ref[:, g*DH:(g+1)*DH] for g in range(QHEADS)], axis=0)
    k = kv[h, :, :, :DH].reshape(keys, DH)
    v = kv[h, :, :, DH:].reshape(keys, DH)
    s = lax.dot_general(k, qs, (((1,), (1,)), ((), ())), preferred_element_type=f32)
    top = None
    for j in range(NCTX):
        part = s[j*T:(j+1)*T]
        if j == 0:
            key = lax.broadcasted_iota(jnp.int32, (T, R), 0)
            token = lax.broadcasted_iota(jnp.int32, (T, R), 1) % T
            part = jnp.where(key <= token, part, -jnp.inf)
        else:
            part = jnp.where(j <= c, part, -jnp.inf)
        s_scr[pl.ds(j*T, T), :] = part
        best = jnp.max(part.reshape(T//8, 8, R), axis=0)
        top = best if top is None else jnp.maximum(top, best)
    top = jnp.max(top, axis=0, keepdims=True)

    weights = jnp.exp2((s_scr[...] - top) * (scale * LOG2E))
    total = jnp.sum(jnp.sum(weights.reshape(keys//8, 8, R), axis=0), axis=0, keepdims=True)
    wt_scr[...] = weights.astype(bf16)
    acc = jnp.dot(vt_scr[...], wt_scr[...], preferred_element_type=f32)
    inv = 1.0 / total
    out_t = (acc * inv).astype(bf16).astype(f32)
    do_t = jnp.concatenate([do_ref[:, g*DH:(g+1)*DH].astype(f32).T for g in range(QHEADS)], axis=1)
    dos_t = (do_t * inv).astype(bf16).astype(f32)
    delta = jnp.sum(dos_t * out_t, axis=0, keepdims=True)
    dos = jnp.concatenate([dos_t[:, g*DH:(g+1)*DH].T for g in range(QHEADS)], axis=0).astype(bf16)
    for g in range(QHEADS):
        out_ref[:, g*DH:(g+1)*DH] = out_t[:, g*DH:(g+1)*DH].T.astype(bf16)

    dprobs = lax.dot_general(v, dos, (((1,), (1,)), ((), ())), preferred_element_type=f32)
    wb = wt_scr[...]
    ds = (dprobs - delta).astype(bf16) * wb
    dq = jnp.dot(kt_scr[...], ds, preferred_element_type=f32) * scale
    dk_acc[...] += jnp.dot(ds, qs, preferred_element_type=f32)
    dv_acc[...] += jnp.dot(wb, dos, preferred_element_type=f32)
    for g in range(QHEADS):
        dq_ref[:, g*DH:(g+1)*DH] = dq[:, g*DH:(g+1)*DH].T.astype(bf16)

    step = h * tiles + t

    @pl.when(step == 1)
    def _():
        w_share(1)
        w_arrived(2, 1)
        w_start(2, 2)

    @pl.when(step == 2)
    def _():
        project(1)

    @pl.when(step == 3)
    def _():
        forward_keys(1)
        w_share(2)
        w_arrived(3, 1)
        w_start(3, 2)
        tok_copy.start()
        for j in range(1, NCTX):
            tok_push(j).start()

    @pl.when(step == 4)
    def _():
        project(2)

    @pl.when(step == 5)
    def _():
        w_share(3)

    @pl.when(step == 6)
    def _():
        forward_keys(2)
        project(3)

    @pl.when(step == 9)
    def _():
        forward_keys(3)
        tok_copy.wait()
        for j in range(1, NCTX):
            tok_push(j).wait_recv()

    @pl.when((t == 0) & (h >= 1))
    def _():
        add_pair(h - 1)

    @pl.when((t == 0) & (h >= 2))
    def _():
        forward_grads(h - 2)

    @pl.when((t == 2) & (h >= 1))
    def _():
        finish_block(h - 1)

    @pl.when((t == 2) & (h >= 2))
    def _():
        weight_grad(h - 2)

    @pl.when(t == tiles - 1)
    def _():
        for q in range(CHIPS):
            for parity, ref in ((0, even), (1, odd)):
                rows = pl.ds((2 * q + parity) * T, T)
                ref[h, q, :, :DH] = (dk_acc[rows, :] * scale).astype(bf16)
                ref[h, q, :, DH:] = dv_acc[rows, :].astype(bf16)
        swap(h).start()

    @pl.when((t == tiles - 1) & (h == KVH - 1))
    def _():
        last = KVH - 1
        forward_grads(last - 1)
        add_pair(last)
        weight_grad(last - 1)
        finish_block(last)
        gp = jnp.concatenate([gp_own[2 * hd + u] for hd in range(KVH) for u in range(2)], axis=1)
        block = weight.shape[4] * weight.shape[5] * weight.shape[6] * weight.shape[7]

        def inputs_part(n, carry):
            w = jnp.concatenate([weight[hd, u, n // 2, n % 2].reshape(block, DH)
                                 for hd in range(KVH) for u in range(2)], axis=1)
            gin_ref[:, pl.ds(pl.multiple_of(n * block, block), block)] = lax.dot_general(
                gp, w, (((1,), (1,)), ((), ())), preferred_element_type=f32).astype(bf16)
            return carry

        lax.fori_loop(0, tok_ref.shape[1] // block, inputs_part, 0)
        forward_grads(last)
        weight_grad(last)
        for hd in range(KVH):
            total_w = dw[hd, dp]
            for j in range(1, NDP):
                dw_push(hd, j).wait_recv()
                total_w = total_w + dw_landed[hd, j]
            gw_ref[:, hd*DH:(hd+1)*DH] = total_w[:, :DH]
            gw_ref[:, (KVH+hd)*DH:(KVH+hd+1)*DH] = total_w[:, DH:]
        for hd in range(KVH):
            for u in range(2):
                for phase in range(3):
                    for k in (1, 2, 3):
                        w_push(hd, u, phase, k).wait_send()
                w_swap(hd, u).wait_send()
            for i in far:
                @pl.when(chip + i < CHIPS)
                def _():
                    kv_push(hd, i).wait_send()

                @pl.when(i <= chip)
                def _():
                    kv_forward(hd, i).wait_send()
                    sum_push(hd, i).wait_send()

                gp_push(hd, i).wait_send()

            @pl.when(core == 0)
            def _():
                kv_own(hd).wait_send()

            swap(hd).wait_send()
            for i in range(CHIPS):
                gp_forward(hd, i).wait_send()
            for j in range(1, NDP):
                dw_push(hd, j).wait_send()
        for j in range(1, NCTX):
            tok_push(j).wait_send()


def main(q, do, tokens, weight, cosine, sine):
    tiles = q.shape[1] // DH // KVH // QHEADS
    keys, R = NCTX * T, QHEADS * T
    tile = pl.BlockSpec((T, R), lambda h, t: (0, h * tiles + t))

    def whole(array):
        return pl.BlockSpec(array.shape, lambda h, t: (0, 0))

    features = tokens.shape[1]
    rows, width = weight.shape
    dma = pltpu.SemaphoreType.DMA
    shared = pltpu.VMEM((KVH, CHIPS, T, 2 * DH), bf16)
    return pl.pallas_call(
        functools.partial(main_kernel, tiles),
        grid=(KVH, tiles),
        in_specs=[tile, tile, whole(tokens), whole(weight), whole(cosine), whole(sine)],
        out_specs=[tile, tile,
                   pl.BlockSpec((T, features), lambda h, t: (0, 0)),
                   pl.BlockSpec((rows, width), lambda h, t: (0, 0))],
        out_shape=[jax.ShapeDtypeStruct(q.shape, bf16), jax.ShapeDtypeStruct(q.shape, bf16),
                   jax.ShapeDtypeStruct((T, features), bf16), jax.ShapeDtypeStruct((rows, width), f32)],
        scratch_shapes=[
            pltpu.VMEM((KVH, NCTX, T, 2 * DH), bf16),
            pltpu.VMEM((keys, R), f32), pltpu.VMEM((keys, R), bf16),
            pltpu.VMEM((DH, keys), bf16), pltpu.VMEM((DH, keys), bf16),
            pltpu.VMEM((keys, DH), f32), pltpu.VMEM((keys, DH), f32),
            shared, shared, shared, shared,
            pltpu.VMEM((T, 2 * DH), f32),
            pltpu.VMEM((KVH, NCTX, T, 2 * DH), bf16),
            pltpu.VMEM((2 * KVH, T, DH), bf16),
            pltpu.VMEM((KVH, 2, 4, 2, 4, 2, 2, rows, DH), bf16),
            pltpu.VMEM((NDP, NCTX, rows, T), bf16), pltpu.VMEM((NDP, rows, keys), bf16),
            pltpu.VMEM((KVH, NDP, rows, 2 * DH), f32), pltpu.VMEM((KVH, NDP, rows, 2 * DH), f32),
            dma((KVH * 18,)), dma((KVH * 18,)), dma((KVH, 2)), dma((KVH, 2)), dma,
            dma((KVH, CHIPS)), dma((KVH, CHIPS)), dma((KVH, CHIPS)), dma((KVH, CHIPS)),
            dma((KVH,)), dma((KVH,)), dma((KVH, CHIPS)), dma((KVH, CHIPS)),
            dma((KVH, CHIPS)), dma((KVH, CHIPS)), dma((KVH, CHIPS)), dma((KVH, CHIPS)),
            dma((KVH, NDP)), dma((KVH, NDP)), dma((NCTX,)), dma((NCTX,))],
        compiler_params=pltpu.CompilerParams(
            collective_id=0, has_side_effects=True, vmem_limit_bytes=60 * 2**20),
        name="projection_attention_exchanges",
    )(q, do, tokens, weight, cosine, sine)


def on_device(inputs, queries, grad_output, kv_weight):
    count = inputs.shape[1]
    ctx = lax.axis_index("ctx")
    cosine, sine = rope_tables(ctx * count + jnp.arange(count, dtype=jnp.int32), DH)
    attn_out, grad_query, grad_inputs, grad_weight = main(
        queries[0], grad_output[0], inputs[0], kv_weight,
        jnp.concatenate([cosine, cosine], axis=1), jnp.concatenate([sine, -sine], axis=1))
    return (attn_out[None], grad_query[None], grad_inputs[None], grad_weight)


def solution(mesh):
    tokens = P("dp", "ctx", None)
    rows = P(("dp", "ctx"), None)
    return jax.shard_map(
        on_device, mesh=mesh, in_specs=(tokens, tokens, tokens, rows),
        out_specs=(tokens, tokens, tokens, rows), check_vma=False)
```

```python
import functools
import math

import jax
import jax.numpy as jnp
from jax import lax
from jax.experimental import pallas as pl
from jax.experimental.pallas import tpu as pltpu
from jax.sharding import PartitionSpec as P

DH = 128
LOG2E = math.log2(math.e)
ROPE_BASE = 500000.0
MESH = pl.DeviceIdType.MESH
NCTX = 16
CHIPS = NCTX // 2
f32, bf16 = jnp.float32, jnp.bfloat16


def rope_tables(positions, head_dim):
    half_dim = head_dim // 2
    frequency = ROPE_BASE ** (-2.0 * jnp.arange(half_dim, dtype=f32) / head_dim)
    angles = positions.astype(f32)[:, None] * frequency[None, :]
    return jnp.cos(angles), jnp.sin(angles)


def position():
    dp, ctx = lax.axis_index("dp"), lax.axis_index("ctx")
    return dp // 2, dp % 2, ctx // 4, (ctx // 2) % 2, ctx % 2


def device_at(y, zh, x, zl, core):
    return (y * 2 + zh, x * 4 + zl * 2 + core)


def meet(peers):
    barrier = pltpu.get_barrier_semaphore()
    for peer in peers:
        pl.semaphore_signal(barrier, inc=1, device_id=peer, device_id_type=MESH)
    pl.semaphore_wait(barrier, len(peers))


QHEADS = 4
GROUP = 8
SPREAD = 16
KVH = 4
T = 128


def main_kernel(tiles, q_ref, do_ref, tok_ref, w_ref, cos_ref, sin_ref,
                out_ref, dq_ref, gin_ref, gw_ref,
                kv, s_scr, wt_scr, kt_scr, vt_scr, dk_acc, dv_acc,
                even, odd, theirs, landed, own32, gp_all, gp_own, weight, tok_own, tok_t, dw, dw_landed,
                w_send, w_recv, ws_send, ws_recv, tok_local, kv_send, kv_recv, fw_send, fw_recv, swap_send, swap_recv, ps_send, ps_recv,
                ag_send, ag_recv, agf_send, agf_recv, dw_send, dw_recv, a_send, a_recv):
    dp, c = lax.axis_index("dp"), lax.axis_index("ctx")
    chip, core = c // 2, c % 2
    partner = (dp, chip * 2 + 1 - core)
    h, t = pl.program_id(0), pl.program_id(1)
    R = QHEADS * T
    keys = NCTX * T
    scale = DH ** -0.5
    far = list(range(1, CHIPS))
    y, zh, x, zl, _ = position()
    z = zh * 2 + zl

    def chip_at(i):
        return (dp, lax.rem(chip + i + CHIPS, CHIPS) * 2 + core)

    def remote(src, dst, send, recv, device):
        return pltpu.make_async_remote_copy(
            src_ref=src, dst_ref=dst, send_sem=send, recv_sem=recv, device_id=device, device_id_type=MESH)

    def w_axes(hd, u):
        return (("zxy", "yzx"), ("xzy", "yxz"))[hd % 2][u]

    def along(axis, step):
        if axis == "x":
            return device_at(y, zh, lax.rem(x + step, 4), zl, core)
        if axis == "y":
            return device_at(lax.rem(y + step, 4), zh, x, zl, core)
        to = lax.rem(z + step, 4)
        return device_at(y, to // 2, x, lax.rem(to, 2), core)

    def w_region(hd, u, done):
        yy = slice(None) if "y" in done else y
        xx = slice(None) if "x" in done else x
        zz, zzl = (slice(None), slice(None)) if "z" in done else (zh, zl)
        return weight.at[hd, u, yy, zz, xx, zzl, core]

    def w_push(hd, u, phase, step):
        axes = w_axes(hd, u)
        region = w_region(hd, u, axes[:phase])
        n = ((hd * 2 + u) * 3 + phase) * 3 + step - 1
        return remote(region, region, w_send.at[n], w_recv.at[n], along(axes[phase], step))

    def w_start(hd, phase):
        for u in range(2):
            for step in (1, 2, 3):
                w_push(hd, u, phase, step).start()

    def w_arrived(hd, phase):
        for u in range(2):
            for step in (1, 2, 3):
                w_push(hd, u, phase, step).wait_recv()

    def w_swap(hd, u):
        region = w_region(hd, u, "xyz")
        return remote(region, region, ws_send.at[hd, u], ws_recv.at[hd, u], partner)

    def w_share(hd):
        for u in range(2):
            for step in (1, 2, 3):
                w_push(hd, u, 2, step).wait_recv()
            w_swap(hd, u).start()

    def project(hd):
        for u in range(2):
            w_swap(hd, u).wait_recv()
        features = tok_ref.shape[1]
        key_part = jnp.dot(tok_ref[...], weight[hd, 0].reshape(features, DH), preferred_element_type=f32)
        kv[hd, 0, :, :DH] = (key_part * cos_ref[...] - pltpu.roll(key_part, DH // 2, 1) * sin_ref[...]).astype(bf16)
        kv[hd, 0, :, DH:] = jnp.dot(
            tok_ref[...], weight[hd, 1].reshape(features, DH), preferred_element_type=f32).astype(bf16)
        for i in far:
            @pl.when(chip + i < CHIPS)
            def _():
                kv_push(hd, i).start()

        @pl.when(core == 0)
        def _():
            kv_own(hd).start()

    def kv_push(hd, i):
        return remote(kv.at[hd, 0], kv.at[hd, 2 * i], kv_send.at[hd, i], kv_recv.at[hd, i], chip_at(i))

    def kv_own(hd):
        return remote(kv.at[hd, 0], kv.at[hd, 1], fw_send.at[hd, 0], fw_recv.at[hd, 0], partner)

    def kv_forward(hd, i):
        return remote(kv.at[hd, 2 * i], kv.at[hd, 2 * i + 1 - 2 * core], fw_send.at[hd, i], fw_recv.at[hd, i], partner)

    def swap(hd):
        return remote(odd.at[hd], theirs.at[hd], swap_send.at[hd], swap_recv.at[hd], partner)

    def sum_push(hd, i):
        return remote(even.at[hd, i], landed.at[hd, i], ps_send.at[hd, i], ps_recv.at[hd, i], chip_at(-i))

    def gp_push(hd, dy):
        return remote(gp_all.at[hd, 0], gp_all.at[hd, 2 * dy], ag_send.at[hd, dy], ag_recv.at[hd, dy], along("y", dy))

    def gp_forward(hd, dy):
        return remote(gp_all.at[hd, 2 * dy], gp_all.at[hd, 2 * dy + 1],
                      agf_send.at[hd, dy], agf_recv.at[hd, dy], partner)

    def tok_push(j):
        to_y, to_core = lax.rem(y + j // 2, 4), lax.rem(core + j % 2, 2)
        return remote(tok_own.at[to_y, :, :, :, to_core], tok_t.at[:, :, :, :, pl.ds(j * T, T)],
                      a_send.at[j], a_recv.at[j], device_at(to_y, zh, x, zl, to_core))

    def across(j):
        to = lax.rem(z + j % 4, 4)
        return to // 2, lax.rem(x + j // 4, 4), lax.rem(to, 2)

    def dw_push(hd, j):
        to_zh, to_x, to_zl = across(j)
        return remote(dw.at[hd, to_zh, to_x, to_zl], dw_landed.at[hd, j], dw_send.at[hd, j], dw_recv.at[hd, j],
                      device_at(y, to_zh, to_x, to_zl, core))

    tok_copy = pltpu.make_async_copy(tok_own.at[y, :, :, :, core], tok_t.at[:, :, :, :, pl.ds(0, T)], tok_local)

    def forward_keys(hd):
        for i in far:
            @pl.when(i <= chip)
            def _():
                kv_push(hd, i).wait_recv()
                kv_forward(hd, i).start()

    def await_keys(hd):
        for i in far:
            @pl.when(i <= chip)
            def _():
                kv_forward(hd, i).wait_recv()

        @pl.when(core == 1)
        def _():
            kv_own(hd).wait_recv()

    def add_pair(hd):
        swap(hd).wait_recv()
        own32[...] = even[hd, 0].astype(f32) + theirs[hd, lax.rem(CHIPS - core, CHIPS)].astype(f32)
        for i in far:
            @pl.when(i <= chip)
            def _():
                total = even[hd, i].astype(f32) + theirs[hd, i - core].astype(f32)
                even[hd, i] = total.astype(bf16)
                sum_push(hd, i).start()

    def finish_block(hd):
        for i in far:
            @pl.when(chip + i < CHIPS)
            def _():
                sum_push(hd, i).wait_recv()
                own32[...] += landed[hd, i].astype(f32)
        key_part = own32[:, :DH]
        key_part = (key_part * cos_ref[...] + pltpu.roll(key_part, DH // 2, 1) * sin_ref[...]).astype(bf16)
        value_part = own32[:, DH:].astype(bf16)
        gp_all[hd, 0, :, :DH] = key_part
        gp_all[hd, 0, :, DH:] = value_part
        gp_own[2 * hd] = key_part
        gp_own[2 * hd + 1] = value_part
        for dy in (1, 2, 3):
            gp_push(hd, dy).start()
        gp_forward(hd, 0).start()

    def forward_grads(hd):
        for dy in (1, 3, 2):
            gp_push(hd, dy).wait_recv()
            gp_forward(hd, dy).start()

    def weight_grad(hd):
        for dy in range(4):
            gp_forward(hd, dy).wait_recv()
        part = jnp.dot(tok_t[...].reshape(-1, GROUP * T), gp_all[hd].reshape(GROUP * T, 2 * DH),
                       preferred_element_type=f32)
        dw[hd] = part.reshape(dw.shape[1:]).astype(bf16)
        for j in range(1, SPREAD):
            dw_push(hd, j).start()

    @pl.when((h == 0) & (t == 0))
    def _():
        peers = [partner] + [along("y", dy) for dy in (1, 2, 3)]
        peers += [device_at(lax.rem(y + dy, 4), zh, x, zl, 1 - core) for dy in (1, 2, 3)]
        for j in range(1, SPREAD):
            to_zh, to_x, to_zl = across(j)
            peers.append(device_at(y, to_zh, to_x, to_zl, core))
        meet(peers)
        for hd in range(KVH):
            for u in range(2):
                first = (u * KVH + hd) * DH
                weight[hd, u, y, zh, x, zl, core] = w_ref[:, first:first + DH]
        for hd in range(KVH):
            w_start(hd, 0)
        w_arrived(0, 0)
        w_start(0, 1)
        rows = tok_own.shape[5]
        for n in range(tok_ref.shape[1] // T):
            turned = tok_ref[:, n*T:(n+1)*T].T
            for m in range(T // rows):
                g = n * (T // rows) + m
                tok_own[g // 32, g // 16 % 2, g // 4 % 4, g // 2 % 2, g % 2] = turned[m*rows:(m+1)*rows]
        for j in range(1, NCTX):
            @pl.when(j > c)
            def _():
                kv[:, j] = jnp.zeros((KVH, T, 2 * DH), bf16)
        w_arrived(0, 1)
        w_start(0, 2)
        for hd in range(1, KVH):
            w_arrived(hd, 0)
            w_start(hd, 1)
        w_share(0)
        project(0)
        w_arrived(1, 1)
        w_start(1, 2)
        forward_keys(0)

    @pl.when(t == 0)
    def _():
        await_keys(h)
        dk_acc[...] = jnp.zeros_like(dk_acc)
        dv_acc[...] = jnp.zeros_like(dv_acc)
        kt_scr[...] = kv[h, :, :, :DH].reshape(keys, DH).T
        vt_scr[...] = kv[h, :, :, DH:].reshape(keys, DH).T

    qs = jnp.concatenate([q_ref[:, g*DH:(g+1)*DH] for g in range(QHEADS)], axis=0)
    k = kv[h, :, :, :DH].reshape(keys, DH)
    v = kv[h, :, :, DH:].reshape(keys, DH)
    s = lax.dot_general(k, qs, (((1,), (1,)), ((), ())), preferred_element_type=f32)
    top = None
    for j in range(NCTX):
        part = s[j*T:(j+1)*T]
        if j == 0:
            key = lax.broadcasted_iota(jnp.int32, (T, R), 0)
            token = lax.broadcasted_iota(jnp.int32, (T, R), 1) % T
            part = jnp.where(key <= token, part, -jnp.inf)
        else:
            part = jnp.where(j <= c, part, -jnp.inf)
        s_scr[pl.ds(j*T, T), :] = part
        best = jnp.max(part.reshape(T//8, 8, R), axis=0)
        top = best if top is None else jnp.maximum(top, best)
    top = jnp.max(top, axis=0, keepdims=True)

    weights = jnp.exp2((s_scr[...] - top) * (scale * LOG2E))
    total = jnp.sum(jnp.sum(weights.reshape(keys//8, 8, R), axis=0), axis=0, keepdims=True)
    wt_scr[...] = weights.astype(bf16)
    acc = jnp.dot(vt_scr[...], wt_scr[...], preferred_element_type=f32)
    inv = 1.0 / total
    out_t = (acc * inv).astype(bf16).astype(f32)
    do_t = jnp.concatenate([do_ref[:, g*DH:(g+1)*DH].astype(f32).T for g in range(QHEADS)], axis=1)
    dos_t = (do_t * inv).astype(bf16).astype(f32)
    delta = jnp.sum(dos_t * out_t, axis=0, keepdims=True)
    dos = jnp.concatenate([dos_t[:, g*DH:(g+1)*DH].T for g in range(QHEADS)], axis=0).astype(bf16)
    for g in range(QHEADS):
        out_ref[:, g*DH:(g+1)*DH] = out_t[:, g*DH:(g+1)*DH].T.astype(bf16)

    dprobs = lax.dot_general(v, dos, (((1,), (1,)), ((), ())), preferred_element_type=f32)
    wb = wt_scr[...]
    ds = (dprobs - delta).astype(bf16) * wb
    dq = jnp.dot(kt_scr[...], ds, preferred_element_type=f32) * scale
    dk_acc[...] += jnp.dot(ds, qs, preferred_element_type=f32)
    dv_acc[...] += jnp.dot(wb, dos, preferred_element_type=f32)
    for g in range(QHEADS):
        dq_ref[:, g*DH:(g+1)*DH] = dq[:, g*DH:(g+1)*DH].T.astype(bf16)

    step = h * tiles + t

    @pl.when(step == 1)
    def _():
        w_share(1)
        w_arrived(2, 1)
        w_start(2, 2)

    @pl.when(step == 2)
    def _():
        project(1)

    @pl.when(step == 3)
    def _():
        forward_keys(1)
        w_share(2)
        w_arrived(3, 1)
        w_start(3, 2)
        tok_copy.start()
        for j in range(1, GROUP):
            tok_push(j).start()

    @pl.when(step == 4)
    def _():
        project(2)

    @pl.when(step == 5)
    def _():
        w_share(3)

    @pl.when(step == 6)
    def _():
        forward_keys(2)
        project(3)

    @pl.when(step == 9)
    def _():
        forward_keys(3)
        tok_copy.wait()
        for j in range(1, GROUP):
            tok_push(j).wait_recv()

    @pl.when((t == 0) & (h >= 1))
    def _():
        add_pair(h - 1)

    @pl.when((t == 0) & (h >= 2))
    def _():
        forward_grads(h - 2)

    @pl.when((t == 2) & (h >= 1))
    def _():
        finish_block(h - 1)

    @pl.when((t == 2) & (h >= 2))
    def _():
        weight_grad(h - 2)

    @pl.when(t == tiles - 1)
    def _():
        for q in range(CHIPS):
            for parity, ref in ((0, even), (1, odd)):
                rows = pl.ds((2 * q + parity) * T, T)
                ref[h, q, :, :DH] = (dk_acc[rows, :] * scale).astype(bf16)
                ref[h, q, :, DH:] = dv_acc[rows, :].astype(bf16)
        swap(h).start()

    @pl.when((t == tiles - 1) & (h == KVH - 1))
    def _():
        last = KVH - 1
        forward_grads(last - 1)
        add_pair(last)
        weight_grad(last - 1)
        finish_block(last)
        gp = jnp.concatenate([gp_own[2 * hd + u] for hd in range(KVH) for u in range(2)], axis=1)
        block = weight.shape[4] * weight.shape[5] * weight.shape[6] * weight.shape[7]

        def inputs_part(n, carry):
            w = jnp.concatenate([weight[hd, u, n // 2, n % 2].reshape(block, DH)
                                 for hd in range(KVH) for u in range(2)], axis=1)
            gin_ref[:, pl.ds(pl.multiple_of(n * block, block), block)] = lax.dot_general(
                gp, w, (((1,), (1,)), ((), ())), preferred_element_type=f32).astype(bf16)
            return carry

        lax.fori_loop(0, tok_ref.shape[1] // block, inputs_part, 0)
        forward_grads(last)
        weight_grad(last)
        for hd in range(KVH):
            total_w = dw[hd, zh, x, zl].astype(f32)
            for j in range(1, SPREAD):
                dw_push(hd, j).wait_recv()
                total_w = total_w + dw_landed[hd, j].astype(f32)
            gw_ref[:, hd*DH:(hd+1)*DH] = total_w[:, :DH]
            gw_ref[:, (KVH+hd)*DH:(KVH+hd+1)*DH] = total_w[:, DH:]
        for hd in range(KVH):
            for u in range(2):
                for phase in range(3):
                    for k in (1, 2, 3):
                        w_push(hd, u, phase, k).wait_send()
                w_swap(hd, u).wait_send()
            for i in far:
                @pl.when(chip + i < CHIPS)
                def _():
                    kv_push(hd, i).wait_send()

                @pl.when(i <= chip)
                def _():
                    kv_forward(hd, i).wait_send()
                    sum_push(hd, i).wait_send()

            @pl.when(core == 0)
            def _():
                kv_own(hd).wait_send()

            swap(hd).wait_send()
            for dy in range(4):
                gp_forward(hd, dy).wait_send()
            for dy in (1, 2, 3):
                gp_push(hd, dy).wait_send()
            for j in range(1, SPREAD):
                dw_push(hd, j).wait_send()
        for j in range(1, GROUP):
            tok_push(j).wait_send()


def main(q, do, tokens, weight, cosine, sine):
    tiles = q.shape[1] // DH // KVH // QHEADS
    keys, R = NCTX * T, QHEADS * T
    tile = pl.BlockSpec((T, R), lambda h, t: (0, h * tiles + t))

    def whole(array):
        return pl.BlockSpec(array.shape, lambda h, t: (0, 0))

    features = tokens.shape[1]
    rows, width = weight.shape
    dma = pltpu.SemaphoreType.DMA
    shared = pltpu.VMEM((KVH, CHIPS, T, 2 * DH), bf16)
    return pl.pallas_call(
        functools.partial(main_kernel, tiles),
        grid=(KVH, tiles),
        in_specs=[tile, tile, whole(tokens), whole(weight), whole(cosine), whole(sine)],
        out_specs=[tile, tile,
                   pl.BlockSpec((T, features), lambda h, t: (0, 0)),
                   pl.BlockSpec((rows, width), lambda h, t: (0, 0))],
        out_shape=[jax.ShapeDtypeStruct(q.shape, bf16), jax.ShapeDtypeStruct(q.shape, bf16),
                   jax.ShapeDtypeStruct((T, features), bf16), jax.ShapeDtypeStruct((rows, width), f32)],
        scratch_shapes=[
            pltpu.VMEM((KVH, NCTX, T, 2 * DH), bf16),
            pltpu.VMEM((keys, R), f32), pltpu.VMEM((keys, R), bf16),
            pltpu.VMEM((DH, keys), bf16), pltpu.VMEM((DH, keys), bf16),
            pltpu.VMEM((keys, DH), f32), pltpu.VMEM((keys, DH), f32),
            shared, shared, shared, shared,
            pltpu.VMEM((T, 2 * DH), f32),
            pltpu.VMEM((KVH, GROUP, T, 2 * DH), bf16),
            pltpu.VMEM((2 * KVH, T, DH), bf16),
            pltpu.VMEM((KVH, 2, 4, 2, 4, 2, 2, rows, DH), bf16),
            pltpu.VMEM((4, 2, 4, 2, 2, rows, T), bf16), pltpu.VMEM((2, 4, 2, rows, GROUP * T), bf16),
            pltpu.VMEM((KVH, 2, 4, 2, rows, 2 * DH), bf16), pltpu.VMEM((KVH, SPREAD, rows, 2 * DH), bf16),
            dma((KVH * 18,)), dma((KVH * 18,)), dma((KVH, 2)), dma((KVH, 2)), dma,
            dma((KVH, CHIPS)), dma((KVH, CHIPS)), dma((KVH, CHIPS)), dma((KVH, CHIPS)),
            dma((KVH,)), dma((KVH,)), dma((KVH, CHIPS)), dma((KVH, CHIPS)),
            dma((KVH, 4)), dma((KVH, 4)), dma((KVH, 4)), dma((KVH, 4)),
            dma((KVH, SPREAD)), dma((KVH, SPREAD)), dma((GROUP,)), dma((GROUP,))],
        compiler_params=pltpu.CompilerParams(
            collective_id=0, has_side_effects=True, vmem_limit_bytes=60 * 2**20),
        name="projection_attention_exchanges",
    )(q, do, tokens, weight, cosine, sine)


def on_device(inputs, queries, grad_output, kv_weight):
    count = inputs.shape[1]
    ctx = lax.axis_index("ctx")
    cosine, sine = rope_tables(ctx * count + jnp.arange(count, dtype=jnp.int32), DH)
    attn_out, grad_query, grad_inputs, grad_weight = main(
        queries[0], grad_output[0], inputs[0], kv_weight,
        jnp.concatenate([cosine, cosine], axis=1), jnp.concatenate([sine, -sine], axis=1))
    return (attn_out[None], grad_query[None], grad_inputs[None], grad_weight)


def solution(mesh):
    tokens = P("dp", "ctx", None)
    rows = P(("dp", "ctx"), None)
    return jax.shard_map(
        on_device, mesh=mesh, in_specs=(tokens, tokens, tokens, rows),
        out_specs=(tokens, tokens, tokens, rows), check_vma=False)
```

```python
import functools
import math

import jax
import jax.numpy as jnp
from jax import lax
from jax.experimental import pallas as pl
from jax.experimental.pallas import tpu as pltpu
from jax.sharding import PartitionSpec as P

DH = 128
LOG2E = math.log2(math.e)
ROPE_BASE = 500000.0
MESH = pl.DeviceIdType.MESH
NCTX = 16
CHIPS = NCTX // 2
f32, bf16 = jnp.float32, jnp.bfloat16


def rope_tables(positions, head_dim):
    half_dim = head_dim // 2
    frequency = ROPE_BASE ** (-2.0 * jnp.arange(half_dim, dtype=f32) / head_dim)
    angles = positions.astype(f32)[:, None] * frequency[None, :]
    return jnp.cos(angles), jnp.sin(angles)


def position():
    dp, ctx = lax.axis_index("dp"), lax.axis_index("ctx")
    return dp // 2, dp % 2, ctx // 4, (ctx // 2) % 2, ctx % 2


def device_at(y, zh, x, zl, core):
    return (y * 2 + zh, x * 4 + zl * 2 + core)


def meet(peers):
    barrier = pltpu.get_barrier_semaphore()
    for peer in peers:
        pl.semaphore_signal(barrier, inc=1, device_id=peer, device_id_type=MESH)
    pl.semaphore_wait(barrier, len(peers))


QHEADS = 8
GROUP = 8
SPREAD = 16
KVH = 4
T = 128


def main_kernel(tiles, q_ref, do_ref, tok_ref, w_ref, cos_ref, sin_ref,
                out_ref, dq_ref, gin_ref, gw_ref,
                kv, s_scr, wt_scr, kt_scr, vt_scr, dk_acc, dv_acc,
                even, odd, theirs, landed, own32, gp_all, gp_own, weight, tok_own, tok_t, dw, dw_landed, gin_acc,
                w_send, w_recv, ws_send, ws_recv, tok_local, kv_send, kv_recv, fw_send, fw_recv, swap_send, swap_recv, ps_send, ps_recv,
                ag_send, ag_recv, agf_send, agf_recv, dw_send, dw_recv, a_send, a_recv):
    dp, c = lax.axis_index("dp"), lax.axis_index("ctx")
    chip, core = c // 2, c % 2
    partner = (dp, chip * 2 + 1 - core)
    h, t = pl.program_id(0), pl.program_id(1)
    R = QHEADS * T
    keys = NCTX * T
    scale = DH ** -0.5
    far = list(range(1, CHIPS))
    y, zh, x, zl, _ = position()
    z = zh * 2 + zl

    def chip_at(i):
        return (dp, lax.rem(chip + i + CHIPS, CHIPS) * 2 + core)

    def remote(src, dst, send, recv, device):
        return pltpu.make_async_remote_copy(
            src_ref=src, dst_ref=dst, send_sem=send, recv_sem=recv, device_id=device, device_id_type=MESH)

    def w_units(hd, u):
        if hd == 0:
            return ((0, 16, ("zxy", "xyz")[u]), (16, 16, ("yzx", "zxy")[u]))
        return ((0, 32, (("zxy", "yzx"), ("xzy", "yxz"))[hd % 2][u]),)

    def along(axis, step):
        if axis == "x":
            return device_at(y, zh, lax.rem(x + step, 4), zl, core)
        if axis == "y":
            return device_at(lax.rem(y + step, 4), zh, x, zl, core)
        to = lax.rem(z + step, 4)
        return device_at(y, to // 2, x, lax.rem(to, 2), core)

    def w_region(hd, u, unit, phase):
        first, count, axes = unit
        done = axes[:phase]
        yy = slice(None) if "y" in done else y
        xx = slice(None) if "x" in done else x
        zz, zzl = (slice(None), slice(None)) if "z" in done else (zh, zl)
        return weight.at[hd, u, yy, zz, xx, zzl, core, pl.ds(first, count)]

    def w_push(hd, u, unit, phase, step):
        region = w_region(hd, u, unit, phase)
        n = (((hd * 2 + u) * 2 + unit[0] // 16) * 3 + phase) * 3 + step - 1
        return remote(region, region, w_send.at[n], w_recv.at[n], along(unit[2][phase], step))

    def w_start(hd, phase, us=(0, 1)):
        for u in us:
            for unit in w_units(hd, u):
                for step in (2, 1, 3):
                    w_push(hd, u, unit, phase, step).start()

    def w_arrived(hd, phase, us=(0, 1)):
        for u in us:
            for unit in w_units(hd, u):
                for step in (1, 3, 2):
                    w_push(hd, u, unit, phase, step).wait_recv()

    def w_swap(hd, u, unit):
        region = w_region(hd, u, unit, 3)
        n = (hd * 2 + u) * 2 + unit[0] // 16
        return remote(region, region, ws_send.at[n], ws_recv.at[n], partner)

    def w_share(hd, us=(0, 1)):
        for u in us:
            for unit in w_units(hd, u):
                for step in (1, 3, 2):
                    w_push(hd, u, unit, 2, step).wait_recv()
                w_swap(hd, u, unit).start()

    def project(hd, us=(0, 1)):
        for u in us:
            for unit in w_units(hd, u):
                w_swap(hd, u, unit).wait_recv()
            part = jnp.dot(tok_ref[...], weight[hd, u].reshape(tok_ref.shape[1], DH), preferred_element_type=f32)
            if u == 0:
                part = part * cos_ref[...] - pltpu.roll(part, DH // 2, 1) * sin_ref[...]
            kv[hd, u, 0] = part.astype(bf16)
            for i in far:
                @pl.when(chip + i < CHIPS)
                def _():
                    kv_push(hd, u, i).start()

            @pl.when(core == 0)
            def _():
                kv_own(hd, u).start()

    def kv_push(hd, u, i):
        return remote(kv.at[hd, u, 0], kv.at[hd, u, 2 * i],
                      kv_send.at[hd, u, i], kv_recv.at[hd, u, i], chip_at(i))

    def kv_own(hd, u):
        return remote(kv.at[hd, u, 0], kv.at[hd, u, 1], fw_send.at[hd, u, 0], fw_recv.at[hd, u, 0], partner)

    def kv_forward(hd, u, i):
        return remote(kv.at[hd, u, 2 * i], kv.at[hd, u, 2 * i + 1 - 2 * core],
                      fw_send.at[hd, u, i], fw_recv.at[hd, u, i], partner)

    def swap(hd):
        return remote(odd.at[hd], theirs.at[hd], swap_send.at[hd], swap_recv.at[hd], partner)

    def sum_push(hd, i):
        return remote(even.at[hd, i], landed.at[hd, i], ps_send.at[hd, i], ps_recv.at[hd, i], chip_at(-i))

    def gp_push(hd, dy):
        return remote(gp_all.at[hd, 0], gp_all.at[hd, 2 * dy], ag_send.at[hd, dy], ag_recv.at[hd, dy], along("y", dy))

    def gp_forward(hd, dy):
        return remote(gp_all.at[hd, 2 * dy], gp_all.at[hd, 2 * dy + 1],
                      agf_send.at[hd, dy], agf_recv.at[hd, dy], partner)

    def tok_push(j):
        to_y, to_core = lax.rem(y + j // 2, 4), lax.rem(core + j % 2, 2)
        return remote(tok_own.at[to_y, :, :, :, to_core], tok_t.at[:, :, :, :, pl.ds(j * T, T)],
                      a_send.at[j], a_recv.at[j], device_at(to_y, zh, x, zl, to_core))

    def across(j):
        to = lax.rem(z + j % 4, 4)
        return to // 2, lax.rem(x + j // 4, 4), lax.rem(to, 2)

    def dw_push(hd, j):
        to_zh, to_x, to_zl = across(j)
        return remote(dw.at[hd, to_zh, to_x, to_zl], dw_landed.at[hd, j], dw_send.at[hd, j], dw_recv.at[hd, j],
                      device_at(y, to_zh, to_x, to_zl, core))

    tok_copy = pltpu.make_async_copy(tok_own.at[y, :, :, :, core], tok_t.at[:, :, :, :, pl.ds(0, T)], tok_local)

    def forward_keys(hd, us=(0, 1)):
        for u in us:
            for i in far:
                @pl.when(i <= chip)
                def _():
                    kv_push(hd, u, i).wait_recv()
                    kv_forward(hd, u, i).start()

    def await_keys(hd, u):
        for i in far:
            @pl.when(i <= chip)
            def _():
                kv_forward(hd, u, i).wait_recv()

        @pl.when(core == 1)
        def _():
            kv_own(hd, u).wait_recv()

    def add_pair(hd):
        swap(hd).wait_recv()
        own32[...] = even[hd, 0].astype(f32) + theirs[hd, lax.rem(CHIPS - core, CHIPS)].astype(f32)
        for i in far:
            @pl.when(i <= chip)
            def _():
                total = even[hd, i].astype(f32) + theirs[hd, i - core].astype(f32)
                even[hd, i] = total.astype(bf16)
                sum_push(hd, i).start()

    def finish_block(hd):
        for i in far:
            @pl.when(chip + i < CHIPS)
            def _():
                sum_push(hd, i).wait_recv()
                own32[...] += landed[hd, i].astype(f32)
        key_part = own32[:, :DH]
        key_part = (key_part * cos_ref[...] + pltpu.roll(key_part, DH // 2, 1) * sin_ref[...]).astype(bf16)
        value_part = own32[:, DH:].astype(bf16)
        gp_all[hd, 0, :, :DH] = key_part
        gp_all[hd, 0, :, DH:] = value_part
        gp_own[2 * hd] = key_part
        gp_own[2 * hd + 1] = value_part
        for dy in (1, 2, 3):
            gp_push(hd, dy).start()
        gp_forward(hd, 0).start()

    def forward_grads(hd):
        for dy in (1, 3, 2):
            gp_push(hd, dy).wait_recv()
            gp_forward(hd, dy).start()

    def weight_grad(hd):
        for dy in range(4):
            gp_forward(hd, dy).wait_recv()
        part = jnp.dot(tok_t[...].reshape(-1, GROUP * T), gp_all[hd].reshape(GROUP * T, 2 * DH),
                       preferred_element_type=f32)
        dw[hd] = part.reshape(dw.shape[1:]).astype(bf16)
        for j in range(1, SPREAD):
            dw_push(hd, j).start()

    @pl.when((h == 0) & (t == 0))
    def _():
        peers = [partner] + [along("y", dy) for dy in (1, 2, 3)]
        peers += [device_at(lax.rem(y + dy, 4), zh, x, zl, 1 - core) for dy in (1, 2, 3)]
        for j in range(1, SPREAD):
            to_zh, to_x, to_zl = across(j)
            peers.append(device_at(y, to_zh, to_x, to_zl, core))
        meet(peers)
        for hd in range(KVH):
            for u in range(2):
                first = (u * KVH + hd) * DH
                weight[hd, u, y, zh, x, zl, core] = w_ref[:, first:first + DH]
        for u in range(2):
            w_start(0, 0, (u,))
        for phase in range(2):
            for u in range(2):
                w_arrived(0, phase, (u,))
                w_start(0, phase + 1, (u,))
        for hd in range(1, KVH):
            w_start(hd, 0)
        rows = tok_own.shape[5]
        for n in range(tok_ref.shape[1] // T):
            turned = tok_ref[:, n*T:(n+1)*T].T
            for m in range(T // rows):
                g = n * (T // rows) + m
                tok_own[g // 32, g // 16 % 2, g // 4 % 4, g // 2 % 2, g % 2] = turned[m*rows:(m+1)*rows]
        w_share(0, (0,))
        w_share(0, (1,))
        project(0, (0,))
        project(0, (1,))
        for hd in range(1, KVH):
            w_arrived(hd, 0)
            w_start(hd, 1)
        for j in range(1, NCTX):
            @pl.when(j > c)
            def _():
                kv[:, :, j] = jnp.zeros((KVH, 2, T, DH), bf16)
        forward_keys(0, (0,))
        w_arrived(1, 1)
        w_start(1, 2)
        forward_keys(0, (1,))

    @pl.when(t == 0)
    def _():
        await_keys(h, 0)
        dk_acc[...] = jnp.zeros_like(dk_acc)
        dv_acc[...] = jnp.zeros_like(dv_acc)
        kt_scr[...] = kv[h, 0].reshape(keys, DH).T

    qs = jnp.concatenate([q_ref[:, g*DH:(g+1)*DH] for g in range(QHEADS)], axis=0)
    k = kv[h, 0].reshape(keys, DH)
    s = lax.dot_general(k, qs, (((1,), (1,)), ((), ())), preferred_element_type=f32)
    top = None
    for j in range(NCTX):
        part = s[j*T:(j+1)*T]
        if j == 0:
            key = lax.broadcasted_iota(jnp.int32, (T, R), 0)
            token = lax.broadcasted_iota(jnp.int32, (T, R), 1) % T
            part = jnp.where(key <= token, part, -jnp.inf)
        else:
            part = jnp.where(j <= c, part, -jnp.inf)
        s_scr[pl.ds(j*T, T), :] = part
        best = jnp.max(part.reshape(T//8, 8, R), axis=0)
        top = best if top is None else jnp.maximum(top, best)
    top = jnp.max(top, axis=0, keepdims=True)

    @pl.when(t == 0)
    def _():
        await_keys(h, 1)
        vt_scr[...] = kv[h, 1].reshape(keys, DH).T

    weights = jnp.exp2((s_scr[...] - top) * (scale * LOG2E))
    total = jnp.sum(jnp.sum(weights.reshape(keys//8, 8, R), axis=0), axis=0, keepdims=True)
    wt_scr[...] = weights.astype(bf16)
    acc = jnp.dot(vt_scr[...], wt_scr[...], preferred_element_type=f32)
    inv = 1.0 / total
    out_t = (acc * inv).astype(bf16).astype(f32)
    do_t = jnp.concatenate([do_ref[:, g*DH:(g+1)*DH].astype(f32).T for g in range(QHEADS)], axis=1)
    dos_t = (do_t * inv).astype(bf16).astype(f32)
    delta = jnp.sum(dos_t * out_t, axis=0, keepdims=True)
    dos = jnp.concatenate([dos_t[:, g*DH:(g+1)*DH].T for g in range(QHEADS)], axis=0).astype(bf16)
    for g in range(QHEADS):
        out_ref[:, g*DH:(g+1)*DH] = out_t[:, g*DH:(g+1)*DH].T.astype(bf16)

    step = h * tiles + t

    @pl.when(step == 1)
    def _():
        project(1)

    @pl.when((t == 0) & (h >= 1))
    def _():
        add_pair(h - 1)

    @pl.when(step == 2)
    def _():
        project(2)

    @pl.when(step == 3)
    def _():
        forward_keys(2)
        project(3)

    @pl.when((t == 0) & (h >= 2))
    def _():
        forward_grads(h - 2)

    @pl.when((t == 1) & (h >= 1))
    def _():
        finish_block(h - 1)

    @pl.when((t == 1) & (h >= 2))
    def _():
        weight_grad(h - 2)

    dprobs = lax.dot_general(kv[h, 1].reshape(keys, DH), dos, (((1,), (1,)), ((), ())), preferred_element_type=f32)
    wb = wt_scr[...]
    ds = (dprobs - delta).astype(bf16) * wb
    dq = jnp.dot(kt_scr[...], ds, preferred_element_type=f32) * scale
    dk_acc[...] += jnp.dot(ds, qs, preferred_element_type=f32)
    dv_acc[...] += jnp.dot(wb, dos, preferred_element_type=f32)
    for g in range(QHEADS):
        dq_ref[:, g*DH:(g+1)*DH] = dq[:, g*DH:(g+1)*DH].T.astype(bf16)

    @pl.when(step == 0)
    def _():
        w_share(1)
        w_arrived(2, 1)
        w_start(2, 2)

    @pl.when(step == 1)
    def _():
        forward_keys(1)
        w_share(2)
        w_arrived(3, 1)
        w_start(3, 2)
        tok_copy.start()
        for j in range(1, GROUP):
            tok_push(j).start()

    @pl.when(step == 2)
    def _():
        w_share(3)

    @pl.when(step == 4)
    def _():
        forward_keys(3)
        tok_copy.wait()
        for j in range(1, GROUP):
            tok_push(j).wait_recv()

    @pl.when(t == tiles - 1)
    def _():
        for q in range(CHIPS):
            for parity, ref in ((0, even), (1, odd)):
                rows = pl.ds((2 * q + parity) * T, T)
                ref[h, q, :, :DH] = (dk_acc[rows, :] * scale).astype(bf16)
                ref[h, q, :, DH:] = dv_acc[rows, :].astype(bf16)
        swap(h).start()

    @pl.when((t == tiles - 1) & (h == KVH - 1))
    def _():
        last = KVH - 1
        forward_grads(last - 1)
        add_pair(last)
        weight_grad(last - 1)
        block = weight.shape[4] * weight.shape[5] * weight.shape[6] * weight.shape[7]

        def inputs_part(heads):
            gp = jnp.concatenate([gp_own[2 * hd + u] for hd in heads for u in range(2)], axis=1)
            for n in range(tok_ref.shape[1] // block):
                w = jnp.concatenate([weight[hd, u, n // 2, n % 2].reshape(block, DH)
                                     for hd in heads for u in range(2)], axis=1)
                yield slice(n * block, (n + 1) * block), lax.dot_general(
                    gp, w, (((1,), (1,)), ((), ())), preferred_element_type=f32)

        for columns, part in inputs_part(range(last)):
            gin_acc[:, columns] = part
        finish_block(last)
        for columns, part in inputs_part([last]):
            gin_ref[:, columns] = (gin_acc[:, columns] + part).astype(bf16)
        forward_grads(last)
        weight_grad(last)
        for hd in range(KVH):
            total_w = dw[hd, zh, x, zl].astype(f32)
            for j in range(1, SPREAD):
                dw_push(hd, j).wait_recv()
                total_w = total_w + dw_landed[hd, j].astype(f32)
            gw_ref[:, hd*DH:(hd+1)*DH] = total_w[:, :DH]
            gw_ref[:, (KVH+hd)*DH:(KVH+hd+1)*DH] = total_w[:, DH:]
        for hd in range(KVH):
            for u in range(2):
                for unit in w_units(hd, u):
                    for phase in range(3):
                        for k in (1, 2, 3):
                            w_push(hd, u, unit, phase, k).wait_send()
                    w_swap(hd, u, unit).wait_send()
            for i in far:
                @pl.when(chip + i < CHIPS)
                def _():
                    for u in range(2):
                        kv_push(hd, u, i).wait_send()

                @pl.when(i <= chip)
                def _():
                    for u in range(2):
                        kv_forward(hd, u, i).wait_send()
                    sum_push(hd, i).wait_send()

            @pl.when(core == 0)
            def _():
                for u in range(2):
                    kv_own(hd, u).wait_send()

            swap(hd).wait_send()
            for dy in range(4):
                gp_forward(hd, dy).wait_send()
            for dy in (1, 2, 3):
                gp_push(hd, dy).wait_send()
            for j in range(1, SPREAD):
                dw_push(hd, j).wait_send()
        for j in range(1, GROUP):
            tok_push(j).wait_send()


def main(q, do, tokens, weight, cosine, sine):
    tiles = q.shape[1] // DH // KVH // QHEADS
    keys, R = NCTX * T, QHEADS * T
    tile = pl.BlockSpec((T, R), lambda h, t: (0, h * tiles + t))

    def whole(array):
        return pl.BlockSpec(array.shape, lambda h, t: (0, 0))

    features = tokens.shape[1]
    rows, width = weight.shape
    dma = pltpu.SemaphoreType.DMA
    shared = pltpu.VMEM((KVH, CHIPS, T, 2 * DH), bf16)
    return pl.pallas_call(
        functools.partial(main_kernel, tiles),
        grid=(KVH, tiles),
        in_specs=[tile, tile, whole(tokens), whole(weight), whole(cosine), whole(sine)],
        out_specs=[tile, tile,
                   pl.BlockSpec((T, features), lambda h, t: (0, 0)),
                   pl.BlockSpec((rows, width), lambda h, t: (0, 0))],
        out_shape=[jax.ShapeDtypeStruct(q.shape, bf16), jax.ShapeDtypeStruct(q.shape, bf16),
                   jax.ShapeDtypeStruct((T, features), bf16), jax.ShapeDtypeStruct((rows, width), f32)],
        scratch_shapes=[
            pltpu.VMEM((KVH, 2, NCTX, T, DH), bf16),
            pltpu.VMEM((keys, R), f32), pltpu.VMEM((keys, R), bf16),
            pltpu.VMEM((DH, keys), bf16), pltpu.VMEM((DH, keys), bf16),
            pltpu.VMEM((keys, DH), f32), pltpu.VMEM((keys, DH), f32),
            shared, shared, shared, shared,
            pltpu.VMEM((T, 2 * DH), f32),
            pltpu.VMEM((KVH, GROUP, T, 2 * DH), bf16),
            pltpu.VMEM((2 * KVH, T, DH), bf16),
            pltpu.VMEM((KVH, 2, 4, 2, 4, 2, 2, rows, DH), bf16),
            pltpu.VMEM((4, 2, 4, 2, 2, rows, T), bf16), pltpu.VMEM((2, 4, 2, rows, GROUP * T), bf16),
            pltpu.VMEM((KVH, 2, 4, 2, rows, 2 * DH), bf16), pltpu.VMEM((KVH, SPREAD, rows, 2 * DH), bf16),
            pltpu.VMEM((T, features), f32),
            dma((KVH * 36,)), dma((KVH * 36,)), dma((KVH * 4,)), dma((KVH * 4,)), dma,
            dma((KVH, 2, CHIPS)), dma((KVH, 2, CHIPS)), dma((KVH, 2, CHIPS)), dma((KVH, 2, CHIPS)),
            dma((KVH,)), dma((KVH,)), dma((KVH, CHIPS)), dma((KVH, CHIPS)),
            dma((KVH, 4)), dma((KVH, 4)), dma((KVH, 4)), dma((KVH, 4)),
            dma((KVH, SPREAD)), dma((KVH, SPREAD)), dma((GROUP,)), dma((GROUP,))],
        compiler_params=pltpu.CompilerParams(
            collective_id=0, has_side_effects=True, vmem_limit_bytes=60 * 2**20),
        name="projection_attention_exchanges",
    )(q, do, tokens, weight, cosine, sine)


def on_device(inputs, queries, grad_output, kv_weight):
    count = inputs.shape[1]
    ctx = lax.axis_index("ctx")
    cosine, sine = rope_tables(ctx * count + jnp.arange(count, dtype=jnp.int32), DH)
    attn_out, grad_query, grad_inputs, grad_weight = main(
        queries[0], grad_output[0], inputs[0], kv_weight,
        jnp.concatenate([cosine, cosine], axis=1), jnp.concatenate([sine, -sine], axis=1))
    return (attn_out[None], grad_query[None], grad_inputs[None], grad_weight)


def solution(mesh):
    tokens = P("dp", "ctx", None)
    rows = P(("dp", "ctx"), None)
    return jax.shard_map(
        on_device, mesh=mesh, in_specs=(tokens, tokens, tokens, rows),
        out_specs=(tokens, tokens, tokens, rows), check_vma=False)
```

```python
import functools
import math

import jax
import jax.numpy as jnp
from jax import lax
from jax.experimental import pallas as pl
from jax.experimental.pallas import tpu as pltpu
from jax.sharding import PartitionSpec as P

DH = 128
LOG2E = math.log2(math.e)
ROPE_BASE = 500000.0
MESH = pl.DeviceIdType.MESH
NCTX = 16
CHIPS = NCTX // 2
f32, bf16 = jnp.float32, jnp.bfloat16


def rope_tables(positions, head_dim):
    half_dim = head_dim // 2
    frequency = ROPE_BASE ** (-2.0 * jnp.arange(half_dim, dtype=f32) / head_dim)
    angles = positions.astype(f32)[:, None] * frequency[None, :]
    return jnp.cos(angles), jnp.sin(angles)


def position():
    dp, ctx = lax.axis_index("dp"), lax.axis_index("ctx")
    return dp // 2, dp % 2, ctx // 4, (ctx // 2) % 2, ctx % 2


def device_at(y, zh, x, zl, core):
    return (y * 2 + zh, x * 4 + zl * 2 + core)


def meet(peers):
    barrier = pltpu.get_barrier_semaphore()
    for peer in peers:
        pl.semaphore_signal(barrier, inc=1, device_id=peer, device_id_type=MESH)
    pl.semaphore_wait(barrier, len(peers))


QHEADS = 8
GROUP = 8
SPREAD = 16
KVH = 4
T = 128


def main_kernel(tiles, q_ref, do_ref, tok_ref, w_ref, cos_ref, sin_ref,
                out_ref, dq_ref, gin_ref, gw_ref,
                kv, s_scr, wt_scr, kt_scr, vt_scr, dk_acc, dv_acc,
                even, odd, theirs, landed, own32, gp_all, gp_own, weight, tok_own, tok_t, dw, dw_landed, gin_acc,
                w_send, w_recv, ws_send, ws_recv, tok_local, kv_send, kv_recv, fw_send, fw_recv, swap_send, swap_recv, ps_send, ps_recv,
                ag_send, ag_recv, agf_send, agf_recv, dw_send, dw_recv, a_send, a_recv):
    dp, c = lax.axis_index("dp"), lax.axis_index("ctx")
    chip, core = c // 2, c % 2
    partner = (dp, chip * 2 + 1 - core)
    h, t = pl.program_id(0), pl.program_id(1)
    R = QHEADS * T
    keys = NCTX * T
    scale = DH ** -0.5
    far = list(range(1, CHIPS))
    y, zh, x, zl, _ = position()
    z = zh * 2 + zl

    def chip_at(i):
        return (dp, lax.rem(chip + i + CHIPS, CHIPS) * 2 + core)

    def remote(src, dst, send, recv, device):
        return pltpu.make_async_remote_copy(
            src_ref=src, dst_ref=dst, send_sem=send, recv_sem=recv, device_id=device, device_id_type=MESH)

    def w_units(hd, u):
        if hd == 0:
            return ((0, 16, ("zxy", "xyz")[u]), (16, 16, ("yzx", "zxy")[u]))
        return ((0, 32, (("zxy", "yzx"), ("xzy", "yxz"))[hd % 2][u]),)

    def along(axis, step):
        if axis == "x":
            return device_at(y, zh, lax.rem(x + step, 4), zl, core)
        if axis == "y":
            return device_at(lax.rem(y + step, 4), zh, x, zl, core)
        to = lax.rem(z + step, 4)
        return device_at(y, to // 2, x, lax.rem(to, 2), core)

    def w_region(hd, u, unit, phase):
        first, count, axes = unit
        done = axes[:phase]
        yy = slice(None) if "y" in done else y
        xx = slice(None) if "x" in done else x
        zz, zzl = (slice(None), slice(None)) if "z" in done else (zh, zl)
        return weight.at[hd, u, yy, zz, xx, zzl, core, pl.ds(first, count)]

    def w_number(hd, u, unit):
        return 2 * u + unit[0] // 16 if hd == 0 else 2 + 2 * hd + u

    def w_push(hd, u, unit, phase, step):
        region = w_region(hd, u, unit, phase)
        n = w_number(hd, u, unit) * 3 + phase
        return remote(region, region, w_send.at[n], w_recv.at[n], along(unit[2][phase], step))

    def w_three(hd, u, unit, phase):
        first, count, _ = unit
        rest = ((0, 0, 0), (0, slice(None), 0), (slice(None), slice(None), slice(None)))[phase]
        region = weight.at[(hd, u, pl.ds(0, 3)) + rest + (core, pl.ds(first, count))]
        n = w_number(hd, u, unit) * 3 + phase
        return remote(region, region, w_send.at[n], w_recv.at[n], partner)

    def w_start(hd, phase, us=(0, 1)):
        for u in us:
            for unit in w_units(hd, u):
                for step in (2, 1, 3):
                    w_push(hd, u, unit, phase, step).start()

    def w_arrived(hd, phase, us=(0, 1)):
        for u in us:
            for unit in w_units(hd, u):
                w_three(hd, u, unit, phase).wait_recv()

    def w_swap(hd, u, unit):
        region = w_region(hd, u, unit, 3)
        n = w_number(hd, u, unit)
        return remote(region, region, ws_send.at[n], ws_recv.at[n], partner)

    def w_share(hd, us=(0, 1)):
        for u in us:
            for unit in w_units(hd, u):
                w_three(hd, u, unit, 2).wait_recv()
                w_swap(hd, u, unit).start()

    def project(hd, us=(0, 1)):
        for u in us:
            for unit in w_units(hd, u):
                w_swap(hd, u, unit).wait_recv()
            part = jnp.dot(tok_ref[...], weight[hd, u].reshape(tok_ref.shape[1], DH), preferred_element_type=f32)
            if u == 0:
                part = part * cos_ref[...] - pltpu.roll(part, DH // 2, 1) * sin_ref[...]
            kv[hd, u, 0, 0] = part.astype(bf16)
        for i in far:
            @pl.when(chip + i < CHIPS)
            def _():
                kv_push(hd, us, i).start()

    def wait_for(n, stand_in, way):
        for count in far:
            @pl.when(n == count)
            def _():
                getattr(stand_in(count), way)()

    def kv_part(hd, us):
        return hd + 1 if len(us) == 2 else us[0]

    def kv_at(hd, us, parity, slots):
        return kv.at[hd, pl.ds(us[0], len(us)), parity, slots]

    def kv_push(hd, us, i):
        n = kv_part(hd, us)
        return remote(kv_at(hd, us, 0, 0), kv_at(hd, us, 0, i), kv_send.at[n], kv_recv.at[n], chip_at(i))

    def kv_some(hd, us, count):
        n = kv_part(hd, us)
        region = kv_at(hd, us, 0, pl.ds(1, count))
        return remote(region, region, kv_send.at[n], kv_recv.at[n], partner)

    def kv_forward(hd, us, from_core):
        n = kv_part(hd, us)
        here, there = (pl.ds(0, 8), pl.ds(0, 8)) if from_core == 0 else (pl.ds(1, 7), pl.ds(0, 7))
        return remote(kv_at(hd, us, 0, here), kv_at(hd, us, 1, there), fw_send.at[n], fw_recv.at[n], partner)

    def swap(hd):
        return remote(odd.at[hd], theirs.at[hd], swap_send.at[hd], swap_recv.at[hd], partner)

    def sum_push(hd, i):
        return remote(even.at[hd, i], landed.at[hd, i], ps_send.at[hd], ps_recv.at[hd], chip_at(-i))

    def sum_some(hd, count):
        region = landed.at[hd, pl.ds(1, count)]
        return remote(region, region, ps_send.at[hd], ps_recv.at[hd], partner)

    def gp_push(hd, dy):
        return remote(gp_all.at[hd, 0], gp_all.at[hd, dy], ag_send.at[hd], ag_recv.at[hd], along("y", dy))

    def gp_three(hd):
        region = gp_all.at[hd, pl.ds(1, 3)]
        return remote(region, region, ag_send.at[hd], ag_recv.at[hd], partner)

    def gp_forward(hd):
        return remote(gp_all.at[hd, pl.ds(0, 4)], gp_all.at[hd, pl.ds(4, 4)],
                      agf_send.at[hd], agf_recv.at[hd], partner)

    def tok_push(j):
        to_y, to_core = lax.rem(y + j % 4, 4), lax.rem(core + j // 4, 2)
        return remote(tok_own.at[to_y, :, :, :, to_core], tok_t.at[:, :, :, :, pl.ds(j * T, T)],
                      a_send, a_recv, device_at(to_y, zh, x, zl, to_core))

    def tok_all():
        region = tok_t.at[:, :, :, :, pl.ds(T, (GROUP - 1) * T)]
        return remote(region, region, a_send, a_recv, partner)

    def across(j):
        to = lax.rem(z + j % 4, 4)
        return to // 2, lax.rem(x + j // 4, 4), lax.rem(to, 2)

    def dw_push(hd, j):
        to_zh, to_x, to_zl = across(j)
        return remote(dw.at[hd, to_zh, to_x, to_zl], dw_landed.at[hd, j], dw_send.at[hd], dw_recv.at[hd],
                      device_at(y, to_zh, to_x, to_zl, core))

    def dw_all(hd):
        region = dw_landed.at[hd, pl.ds(1, SPREAD - 1)]
        return remote(region, region, dw_send.at[hd], dw_recv.at[hd], partner)

    tok_copy = pltpu.make_async_copy(tok_own.at[y, :, :, :, core], tok_t.at[:, :, :, :, pl.ds(0, T)], tok_local)

    def forward_keys(hd, us=(0, 1)):
        wait_for(chip, lambda count: kv_some(hd, us, count), "wait_recv")
        for k in range(2):
            @pl.when(core == k)
            def _():
                kv_forward(hd, us, k).start()

    def await_keys(hd, us):
        for k in range(2):
            @pl.when(core == k)
            def _():
                kv_forward(hd, us, 1 - k).wait_recv()

    def add_pair(hd):
        swap(hd).wait_recv()
        own32[...] = even[hd, 0].astype(f32) + theirs[hd, lax.rem(CHIPS - core, CHIPS)].astype(f32)
        for i in far:
            @pl.when(i <= chip)
            def _():
                total = even[hd, i].astype(f32) + theirs[hd, i - core].astype(f32)
                even[hd, i] = total.astype(bf16)
                sum_push(hd, i).start()

    def finish_block(hd):
        wait_for(CHIPS - 1 - chip, lambda count: sum_some(hd, count), "wait_recv")
        for i in far:
            @pl.when(chip + i < CHIPS)
            def _():
                own32[...] += landed[hd, i].astype(f32)
        key_part = own32[:, :DH]
        key_part = (key_part * cos_ref[...] + pltpu.roll(key_part, DH // 2, 1) * sin_ref[...]).astype(bf16)
        value_part = own32[:, DH:].astype(bf16)
        gp_all[hd, 0, :, :DH] = key_part
        gp_all[hd, 0, :, DH:] = value_part
        gp_own[2 * hd] = key_part
        gp_own[2 * hd + 1] = value_part
        for dy in (1, 2, 3):
            gp_push(hd, dy).start()

    def forward_grads(hd):
        gp_three(hd).wait_recv()
        gp_forward(hd).start()

    def weight_grad(hd):
        gp_forward(hd).wait_recv()
        part = jnp.dot(tok_t[...].reshape(-1, GROUP * T), gp_all[hd].reshape(GROUP * T, 2 * DH),
                       preferred_element_type=f32)
        dw[hd] = part.reshape(dw.shape[1:]).astype(bf16)
        for j in range(1, SPREAD):
            dw_push(hd, j).start()

    step = h * tiles + t

    @pl.when((h == 0) & (t == 0))
    def _():
        meet([partner] + [along(axis, k) for axis in "xyz" for k in (1, 2, 3)])
        for hd in range(KVH):
            for u in range(2):
                first = (u * KVH + hd) * DH
                weight[hd, u, y, zh, x, zl, core] = w_ref[:, first:first + DH]
        for u in range(2):
            w_start(0, 0, (u,))
        for phase in range(2):
            for u in range(2):
                w_arrived(0, phase, (u,))
                w_start(0, phase + 1, (u,))
        for hd in range(1, KVH):
            w_start(hd, 0)
        rows = tok_own.shape[5]
        for n in range(tok_ref.shape[1] // T):
            turned = tok_ref[:, n*T:(n+1)*T].T
            for m in range(T // rows):
                g = n * (T // rows) + m
                tok_own[g // 32, g // 16 % 2, g // 4 % 4, g // 2 % 2, g % 2] = turned[m*rows:(m+1)*rows]
        w_share(0, (0,))
        w_share(0, (1,))
        project(0, (0,))
        project(0, (1,))
        for hd in range(1, KVH):
            w_arrived(hd, 0)
            w_start(hd, 1)
        for i in far:
            @pl.when(i > chip)
            def _():
                kv[:, :, 0, i] = jnp.zeros((KVH, 2, T, DH), bf16)

        @pl.when(core == 0)
        def _():
            kv[:, :, 1, CHIPS - 1] = jnp.zeros((KVH, 2, T, DH), bf16)

        forward_keys(0, (0,))
        w_arrived(1, 1)
        w_start(1, 2)
        forward_keys(0, (1,))

    @pl.when(t == 0)
    def _():
        @pl.when(h == 0)
        def _():
            await_keys(0, (0,))

        @pl.when(h > 0)
        def _():
            await_keys(h, (0, 1))

        dk_acc[...] = jnp.zeros_like(dk_acc)
        dv_acc[...] = jnp.zeros_like(dv_acc)
        kt_scr[...] = kv[h, 0].reshape(keys, DH).T

    qs = jnp.concatenate([q_ref[:, g*DH:(g+1)*DH] for g in range(QHEADS)], axis=0)
    k = kv[h, 0].reshape(keys, DH)
    s = lax.dot_general(k, qs, (((1,), (1,)), ((), ())), preferred_element_type=f32)
    top = None
    for n in range(NCTX):
        j = 2 * (n % CHIPS) + n // CHIPS
        part = s[n*T:(n+1)*T]
        if j == 0:
            key = lax.broadcasted_iota(jnp.int32, (T, R), 0)
            token = lax.broadcasted_iota(jnp.int32, (T, R), 1) % T
            part = jnp.where(key <= token, part, -jnp.inf)
        else:
            part = jnp.where(j <= c, part, -jnp.inf)
        s_scr[pl.ds(n*T, T), :] = part
        best = jnp.max(part.reshape(T//8, 8, R), axis=0)
        top = best if top is None else jnp.maximum(top, best)
    top = jnp.max(top, axis=0, keepdims=True)

    @pl.when(step == 0)
    def _():
        await_keys(0, (1,))

    @pl.when(t == 0)
    def _():
        vt_scr[...] = kv[h, 1].reshape(keys, DH).T

    weights = jnp.exp2((s_scr[...] - top) * (scale * LOG2E))
    total = jnp.sum(jnp.sum(weights.reshape(keys//8, 8, R), axis=0), axis=0, keepdims=True)
    wt_scr[...] = weights.astype(bf16)
    acc = jnp.dot(vt_scr[...], wt_scr[...], preferred_element_type=f32)
    inv = 1.0 / total
    out_t = (acc * inv).astype(bf16).astype(f32)
    do_t = jnp.concatenate([do_ref[:, g*DH:(g+1)*DH].astype(f32).T for g in range(QHEADS)], axis=1)
    dos_t = (do_t * inv).astype(bf16).astype(f32)
    delta = jnp.sum(dos_t * out_t, axis=0, keepdims=True)
    dos = jnp.concatenate([dos_t[:, g*DH:(g+1)*DH].T for g in range(QHEADS)], axis=0).astype(bf16)
    for g in range(QHEADS):
        out_ref[:, g*DH:(g+1)*DH] = out_t[:, g*DH:(g+1)*DH].T.astype(bf16)


    @pl.when(step == 1)
    def _():
        project(1)

    @pl.when((t == 0) & (h >= 1))
    def _():
        add_pair(h - 1)

    @pl.when(step == 2)
    def _():
        project(2)

    @pl.when(step == 3)
    def _():
        forward_keys(2)
        project(3)

    @pl.when((t == 0) & (h >= 2))
    def _():
        forward_grads(h - 2)

    @pl.when((t == 1) & (h >= 1))
    def _():
        finish_block(h - 1)

    @pl.when((t == 1) & (h >= 2))
    def _():
        weight_grad(h - 2)

    dprobs = lax.dot_general(kv[h, 1].reshape(keys, DH), dos, (((1,), (1,)), ((), ())), preferred_element_type=f32)
    wb = wt_scr[...]
    ds = (dprobs - delta).astype(bf16) * wb
    dq = jnp.dot(kt_scr[...], ds, preferred_element_type=f32) * scale
    dk_acc[...] += jnp.dot(ds, qs, preferred_element_type=f32)
    dv_acc[...] += jnp.dot(wb, dos, preferred_element_type=f32)
    for g in range(QHEADS):
        dq_ref[:, g*DH:(g+1)*DH] = dq[:, g*DH:(g+1)*DH].T.astype(bf16)

    @pl.when(step == 0)
    def _():
        w_share(1)
        w_arrived(2, 1)
        w_start(2, 2)

    @pl.when(step == 1)
    def _():
        forward_keys(1)
        w_share(2)
        w_arrived(3, 1)
        w_start(3, 2)
        tok_copy.start()
        for j in range(1, GROUP):
            tok_push(j).start()

    @pl.when(step == 2)
    def _():
        w_share(3)

    @pl.when(step == 4)
    def _():
        forward_keys(3)
        tok_copy.wait()
        tok_all().wait_recv()

    @pl.when(t == tiles - 1)
    def _():
        for q in range(CHIPS):
            for parity, ref in ((0, even), (1, odd)):
                rows = pl.ds((CHIPS * parity + q) * T, T)
                ref[h, q, :, :DH] = (dk_acc[rows, :] * scale).astype(bf16)
                ref[h, q, :, DH:] = dv_acc[rows, :].astype(bf16)
        swap(h).start()

    @pl.when((t == tiles - 1) & (h == KVH - 1))
    def _():
        last = KVH - 1
        forward_grads(last - 1)
        add_pair(last)
        weight_grad(last - 1)
        block = weight.shape[4] * weight.shape[5] * weight.shape[6] * weight.shape[7]

        def inputs_part(heads):
            gp = jnp.concatenate([gp_own[2 * hd + u] for hd in heads for u in range(2)], axis=1)
            for n in range(tok_ref.shape[1] // block):
                w = jnp.concatenate([weight[hd, u, n // 2, n % 2].reshape(block, DH)
                                     for hd in heads for u in range(2)], axis=1)
                yield slice(n * block, (n + 1) * block), lax.dot_general(
                    gp, w, (((1,), (1,)), ((), ())), preferred_element_type=f32)

        for columns, part in inputs_part(range(last)):
            gin_acc[:, columns] = part
        finish_block(last)
        for columns, part in inputs_part([last]):
            gin_ref[:, columns] = (gin_acc[:, columns] + part).astype(bf16)
        forward_grads(last)
        weight_grad(last)
        for hd in range(KVH):
            total_w = dw[hd, zh, x, zl].astype(f32)
            dw_all(hd).wait_recv()
            for j in range(1, SPREAD):
                total_w = total_w + dw_landed[hd, j].astype(f32)
            gw_ref[:, hd*DH:(hd+1)*DH] = total_w[:, :DH]
            gw_ref[:, (KVH+hd)*DH:(KVH+hd+1)*DH] = total_w[:, DH:]
        for hd in range(KVH):
            for u in range(2):
                for unit in w_units(hd, u):
                    for phase in range(3):
                        w_three(hd, u, unit, phase).wait_send()
                    w_swap(hd, u, unit).wait_send()
            for us in (((0,), (1,)) if hd == 0 else ((0, 1),)):
                wait_for(CHIPS - 1 - chip, lambda count: kv_some(hd, us, count), "wait_send")
                for k in range(2):
                    @pl.when(core == k)
                    def _():
                        kv_forward(hd, us, k).wait_send()
            wait_for(chip, lambda count: sum_some(hd, count), "wait_send")
            swap(hd).wait_send()
            gp_three(hd).wait_send()
            gp_forward(hd).wait_send()
            dw_all(hd).wait_send()
        tok_all().wait_send()


def main(q, do, tokens, weight, cosine, sine):
    tiles = q.shape[1] // DH // KVH // QHEADS
    keys, R = NCTX * T, QHEADS * T
    tile = pl.BlockSpec((T, R), lambda h, t: (0, h * tiles + t))

    def whole(array):
        return pl.BlockSpec(array.shape, lambda h, t: (0, 0))

    features = tokens.shape[1]
    rows, width = weight.shape
    dma = pltpu.SemaphoreType.DMA
    shared = pltpu.VMEM((KVH, CHIPS, T, 2 * DH), bf16)
    return pl.pallas_call(
        functools.partial(main_kernel, tiles),
        grid=(KVH, tiles),
        in_specs=[tile, tile, whole(tokens), whole(weight), whole(cosine), whole(sine)],
        out_specs=[tile, tile,
                   pl.BlockSpec((T, features), lambda h, t: (0, 0)),
                   pl.BlockSpec((rows, width), lambda h, t: (0, 0))],
        out_shape=[jax.ShapeDtypeStruct(q.shape, bf16), jax.ShapeDtypeStruct(q.shape, bf16),
                   jax.ShapeDtypeStruct((T, features), bf16), jax.ShapeDtypeStruct((rows, width), f32)],
        scratch_shapes=[
            pltpu.VMEM((KVH, 2, 2, CHIPS, T, DH), bf16),
            pltpu.VMEM((keys, R), f32), pltpu.VMEM((keys, R), bf16),
            pltpu.VMEM((DH, keys), bf16), pltpu.VMEM((DH, keys), bf16),
            pltpu.VMEM((keys, DH), f32), pltpu.VMEM((keys, DH), f32),
            shared, shared, shared, shared,
            pltpu.VMEM((T, 2 * DH), f32),
            pltpu.VMEM((KVH, GROUP, T, 2 * DH), bf16),
            pltpu.VMEM((2 * KVH, T, DH), bf16),
            pltpu.VMEM((KVH, 2, 4, 2, 4, 2, 2, rows, DH), bf16),
            pltpu.VMEM((4, 2, 4, 2, 2, rows, T), bf16), pltpu.VMEM((2, 4, 2, rows, GROUP * T), bf16),
            pltpu.VMEM((KVH, 2, 4, 2, rows, 2 * DH), bf16), pltpu.VMEM((KVH, SPREAD, rows, 2 * DH), bf16),
            pltpu.VMEM((T, features), f32),
            dma((30,)), dma((30,)), dma((10,)), dma((10,)), dma,
            dma((KVH + 1,)), dma((KVH + 1,)), dma((KVH + 1,)), dma((KVH + 1,)),
            dma((KVH,)), dma((KVH,)), dma((KVH,)), dma((KVH,)),
            dma((KVH,)), dma((KVH,)), dma((KVH,)), dma((KVH,)),
            dma((KVH,)), dma((KVH,)), dma, dma],
        compiler_params=pltpu.CompilerParams(
            collective_id=0, has_side_effects=True, vmem_limit_bytes=60 * 2**20),
        name="projection_attention_exchanges",
    )(q, do, tokens, weight, cosine, sine)


def copy_kernel(*refs):
    sems = refs[-1]
    count = len(refs) // 2
    copies = []
    for src, dst in zip(refs[:count], refs[count:-1]):
        rows = min(32, src.shape[0])
        for first in range(0, src.shape[0], rows):
            part = pl.ds(first, rows)
            copies.append(pltpu.make_async_copy(src.at[part], dst.at[part], sems.at[len(copies)]))
    for copy in copies:
        copy.start()
    for copy in copies:
        copy.wait()


def copy_out(arrays):
    hbm = pl.BlockSpec(memory_space=pl.ANY)
    return pl.pallas_call(
        copy_kernel,
        in_specs=[hbm] * len(arrays), out_specs=[hbm] * len(arrays),
        out_shape=[jax.ShapeDtypeStruct(a.shape, a.dtype) for a in arrays],
        scratch_shapes=[pltpu.SemaphoreType.DMA((16,))],
        compiler_params=pltpu.CompilerParams(vmem_limit_bytes=60 * 2**20),
        name="copy_out",
    )(*arrays)


def on_device(inputs, queries, grad_output, kv_weight):
    count = inputs.shape[1]
    ctx = lax.axis_index("ctx")
    cosine, sine = rope_tables(ctx * count + jnp.arange(count, dtype=jnp.int32), DH)
    attn_out, grad_query, grad_inputs, grad_weight = copy_out(main(
        queries[0], grad_output[0], inputs[0], kv_weight,
        jnp.concatenate([cosine, cosine], axis=1), jnp.concatenate([sine, -sine], axis=1)))
    return (attn_out[None], grad_query[None], grad_inputs[None], grad_weight)


def solution(mesh):
    tokens = P("dp", "ctx", None)
    rows = P(("dp", "ctx"), None)
    return jax.shard_map(
        on_device, mesh=mesh, in_specs=(tokens, tokens, tokens, rows),
        out_specs=(tokens, tokens, tokens, rows), check_vma=False)
```

```python
import functools
import math

import jax
import jax.numpy as jnp
from jax import lax
from jax.experimental import pallas as pl
from jax.experimental.pallas import tpu as pltpu
from jax.sharding import PartitionSpec as P

DH = 128
LOG2E = math.log2(math.e)
ROPE_BASE = 500000.0
MESH = pl.DeviceIdType.MESH
NCTX = 16
CHIPS = NCTX // 2
f32, bf16 = jnp.float32, jnp.bfloat16


def rope_tables(positions, head_dim):
    half_dim = head_dim // 2
    frequency = ROPE_BASE ** (-2.0 * jnp.arange(half_dim, dtype=f32) / head_dim)
    angles = positions.astype(f32)[:, None] * frequency[None, :]
    return jnp.cos(angles), jnp.sin(angles)


def position():
    dp, ctx = lax.axis_index("dp"), lax.axis_index("ctx")
    return dp // 2, dp % 2, ctx // 4, (ctx // 2) % 2, ctx % 2


def device_at(y, zh, x, zl, core):
    return (y * 2 + zh, x * 4 + zl * 2 + core)


def meet(peers):
    barrier = pltpu.get_barrier_semaphore()
    for peer in peers:
        pl.semaphore_signal(barrier, inc=1, device_id=peer, device_id_type=MESH)
    pl.semaphore_wait(barrier, len(peers))


QHEADS = 8
GROUP = 8
SPREAD = 16
KVH = 4
T = 128


def main_kernel(tiles, q_ref, do_ref, tok_ref, w_ref, cos_ref, sin_ref,
                out_ref, dq_ref, gin_ref, gw_ref,
                kv, s_scr, wt_scr, kt_scr, vt_scr, dk_acc, dv_acc,
                even, odd, theirs, landed, own32, gp_all, gp_own, weight, tok_own, tok_t, dw, dw_landed, gin_acc,
                w_send, w_recv, ws_send, ws_recv, tok_local, kv_send, kv_recv, fw_send, fw_recv, swap_send, swap_recv, ps_send, ps_recv,
                ag_send, ag_recv, agf_send, agf_recv, dw_send, dw_recv, a_send, a_recv):
    dp, c = lax.axis_index("dp"), lax.axis_index("ctx")
    chip, core = c // 2, c % 2
    partner = (dp, chip * 2 + 1 - core)
    h, t = pl.program_id(0), pl.program_id(1)
    R = QHEADS * T
    keys = NCTX * T
    scale = DH ** -0.5
    far = list(range(1, CHIPS))
    y, zh, x, zl, _ = position()
    z = zh * 2 + zl

    def chip_at(i):
        return (dp, lax.rem(chip + i + CHIPS, CHIPS) * 2 + core)

    def remote(src, dst, send, recv, device):
        return pltpu.make_async_remote_copy(
            src_ref=src, dst_ref=dst, send_sem=send, recv_sem=recv, device_id=device, device_id_type=MESH)

    def w_units(hd, u):
        if hd == 0:
            return ((0, 16, ("zxy", "xyz")[u]), (16, 16, ("yzx", "zxy")[u]))
        return ((0, 32, (("zxy", "yzx"), ("xzy", "yxz"))[hd % 2][u]),)

    def along(axis, step):
        if axis == "x":
            return device_at(y, zh, lax.rem(x + step, 4), zl, core)
        if axis == "y":
            return device_at(lax.rem(y + step, 4), zh, x, zl, core)
        to = lax.rem(z + step, 4)
        return device_at(y, to // 2, x, lax.rem(to, 2), core)

    def w_region(hd, u, unit, phase):
        first, count, axes = unit
        done = axes[:phase]
        yy = slice(None) if "y" in done else y
        xx = slice(None) if "x" in done else x
        zz, zzl = (slice(None), slice(None)) if "z" in done else (zh, zl)
        return weight.at[hd, u, yy, zz, xx, zzl, core, pl.ds(first, count)]

    def w_number(hd, u, unit):
        return 2 * u + unit[0] // 16 if hd == 0 else 2 + 2 * hd + u

    def w_push(hd, u, unit, phase, step):
        region = w_region(hd, u, unit, phase)
        n = w_number(hd, u, unit) * 3 + phase
        return remote(region, region, w_send.at[n], w_recv.at[n], along(unit[2][phase], step))

    def w_three(hd, u, unit, phase):
        first, count, _ = unit
        rest = ((0, 0, 0), (0, slice(None), 0), (slice(None), slice(None), slice(None)))[phase]
        region = weight.at[(hd, u, pl.ds(0, 3)) + rest + (core, pl.ds(first, count))]
        n = w_number(hd, u, unit) * 3 + phase
        return remote(region, region, w_send.at[n], w_recv.at[n], partner)

    def w_start(hd, phase, us=(0, 1)):
        for u in us:
            for unit in w_units(hd, u):
                for step in (2, 1, 3):
                    w_push(hd, u, unit, phase, step).start()

    def w_arrived(hd, phase, us=(0, 1)):
        for u in us:
            for unit in w_units(hd, u):
                w_three(hd, u, unit, phase).wait_recv()

    def w_swap(hd, u, unit):
        region = w_region(hd, u, unit, 3)
        n = w_number(hd, u, unit)
        return remote(region, region, ws_send.at[n], ws_recv.at[n], partner)

    def w_share(hd, us=(0, 1)):
        for u in us:
            for unit in w_units(hd, u):
                w_three(hd, u, unit, 2).wait_recv()
                w_swap(hd, u, unit).start()

    def project(hd, us=(0, 1)):
        for u in us:
            for unit in w_units(hd, u):
                w_swap(hd, u, unit).wait_recv()
            part = jnp.dot(tok_ref[...], weight[hd, u].reshape(tok_ref.shape[1], DH), preferred_element_type=f32)
            if u == 0:
                part = part * cos_ref[...] - pltpu.roll(part, DH // 2, 1) * sin_ref[...]
            kv[hd, u, 0, 0] = part.astype(bf16)
        for i in far:
            @pl.when(chip + i < CHIPS)
            def _():
                kv_push(hd, us, i).start()

    def wait_for(n, stand_in, way):
        for count in far:
            @pl.when(n == count)
            def _():
                getattr(stand_in(count), way)()

    def kv_part(hd, us):
        return hd + 1 if len(us) == 2 else us[0]

    def kv_at(hd, us, parity, slots):
        return kv.at[hd, pl.ds(us[0], len(us)), parity, slots]

    def kv_push(hd, us, i):
        n = kv_part(hd, us)
        return remote(kv_at(hd, us, 0, 0), kv_at(hd, us, 0, i), kv_send.at[n], kv_recv.at[n], chip_at(i))

    def kv_some(hd, us, count):
        n = kv_part(hd, us)
        region = kv_at(hd, us, 0, pl.ds(1, count))
        return remote(region, region, kv_send.at[n], kv_recv.at[n], partner)

    def kv_forward(hd, us, from_core):
        n = kv_part(hd, us)
        here, there = (pl.ds(0, 8), pl.ds(0, 8)) if from_core == 0 else (pl.ds(1, 7), pl.ds(0, 7))
        return remote(kv_at(hd, us, 0, here), kv_at(hd, us, 1, there), fw_send.at[n], fw_recv.at[n], partner)

    def swap(hd):
        return remote(odd.at[hd], theirs.at[hd], swap_send.at[hd], swap_recv.at[hd], partner)

    def sum_push(hd, i):
        return remote(even.at[hd, i], landed.at[hd, i], ps_send.at[hd], ps_recv.at[hd], chip_at(-i))

    def sum_some(hd, count):
        region = landed.at[hd, pl.ds(1, count)]
        return remote(region, region, ps_send.at[hd], ps_recv.at[hd], partner)

    def gp_push(hd, dy):
        return remote(gp_all.at[hd, 0], gp_all.at[hd, dy], ag_send.at[hd], ag_recv.at[hd], along("y", dy))

    def gp_three(hd):
        region = gp_all.at[hd, pl.ds(1, 3)]
        return remote(region, region, ag_send.at[hd], ag_recv.at[hd], partner)

    def gp_forward(hd):
        return remote(gp_all.at[hd, pl.ds(0, 4)], gp_all.at[hd, pl.ds(4, 4)],
                      agf_send.at[hd], agf_recv.at[hd], partner)

    def tok_push(j):
        to_y, to_core = lax.rem(y + j % 4, 4), lax.rem(core + j // 4, 2)
        return remote(tok_own.at[to_y, :, :, :, to_core], tok_t.at[:, :, :, :, pl.ds(j * T, T)],
                      a_send, a_recv, device_at(to_y, zh, x, zl, to_core))

    def tok_all():
        region = tok_t.at[:, :, :, :, pl.ds(T, (GROUP - 1) * T)]
        return remote(region, region, a_send, a_recv, partner)

    def across(j):
        to = lax.rem(z + j % 4, 4)
        return to // 2, lax.rem(x + j // 4, 4), lax.rem(to, 2)

    def dw_push(hd, j):
        to_zh, to_x, to_zl = across(j)
        return remote(dw.at[hd, to_zh, to_x, to_zl], dw_landed.at[hd, j], dw_send.at[hd], dw_recv.at[hd],
                      device_at(y, to_zh, to_x, to_zl, core))

    def dw_all(hd):
        region = dw_landed.at[hd, pl.ds(1, SPREAD - 1)]
        return remote(region, region, dw_send.at[hd], dw_recv.at[hd], partner)

    tok_copy = pltpu.make_async_copy(tok_own.at[y, :, :, :, core], tok_t.at[:, :, :, :, pl.ds(0, T)], tok_local)

    def forward_keys(hd, us=(0, 1)):
        wait_for(chip, lambda count: kv_some(hd, us, count), "wait_recv")
        for k in range(2):
            @pl.when(core == k)
            def _():
                kv_forward(hd, us, k).start()

    def await_keys(hd, us):
        for k in range(2):
            @pl.when(core == k)
            def _():
                kv_forward(hd, us, 1 - k).wait_recv()

    def add_pair(hd):
        swap(hd).wait_recv()
        own32[...] = even[hd, 0].astype(f32) + theirs[hd, lax.rem(CHIPS - core, CHIPS)].astype(f32)
        for i in far:
            @pl.when(i <= chip)
            def _():
                total = even[hd, i].astype(f32) + theirs[hd, i - core].astype(f32)
                even[hd, i] = total.astype(bf16)
                sum_push(hd, i).start()

    def finish_block(hd):
        wait_for(CHIPS - 1 - chip, lambda count: sum_some(hd, count), "wait_recv")
        for i in far:
            @pl.when(chip + i < CHIPS)
            def _():
                own32[...] += landed[hd, i].astype(f32)
        key_part = own32[:, :DH]
        key_part = (key_part * cos_ref[...] + pltpu.roll(key_part, DH // 2, 1) * sin_ref[...]).astype(bf16)
        value_part = own32[:, DH:].astype(bf16)
        gp_all[hd, 0, :, :DH] = key_part
        gp_all[hd, 0, :, DH:] = value_part
        gp_own[2 * hd] = key_part
        gp_own[2 * hd + 1] = value_part
        for dy in (1, 2, 3):
            gp_push(hd, dy).start()

    def forward_grads(hd):
        gp_three(hd).wait_recv()
        gp_forward(hd).start()

    def weight_grad(hd):
        gp_forward(hd).wait_recv()
        part = jnp.dot(tok_t[...].reshape(-1, GROUP * T), gp_all[hd].reshape(GROUP * T, 2 * DH),
                       preferred_element_type=f32)
        dw[hd] = part.reshape(dw.shape[1:]).astype(bf16)
        for j in range(1, SPREAD):
            dw_push(hd, j).start()

    step = h * tiles + t

    @pl.when((h == 0) & (t == 0))
    def _():
        meet([partner] + [along(axis, k) for axis in "xyz" for k in (1, 2, 3)])
        for hd in range(KVH):
            for u in range(2):
                first = (u * KVH + hd) * DH
                weight[hd, u, y, zh, x, zl, core] = w_ref[:, first:first + DH]
        for u in range(2):
            w_start(0, 0, (u,))
        for phase in range(2):
            for u in range(2):
                w_arrived(0, phase, (u,))
                w_start(0, phase + 1, (u,))
        for hd in range(1, KVH):
            w_start(hd, 0)
        rows = tok_own.shape[5]
        for n in range(tok_ref.shape[1] // T):
            turned = tok_ref[:, n*T:(n+1)*T].T
            for m in range(T // rows):
                g = n * (T // rows) + m
                tok_own[g // 32, g // 16 % 2, g // 4 % 4, g // 2 % 2, g % 2] = turned[m*rows:(m+1)*rows]
        w_share(0, (0,))
        w_share(0, (1,))
        project(0, (0,))
        project(0, (1,))
        for hd in range(1, KVH):
            w_arrived(hd, 0)
            w_start(hd, 1)
        for i in far:
            @pl.when(i > chip)
            def _():
                kv[:, :, 0, i] = jnp.zeros((KVH, 2, T, DH), bf16)

        @pl.when(core == 0)
        def _():
            kv[:, :, 1, CHIPS - 1] = jnp.zeros((KVH, 2, T, DH), bf16)

        forward_keys(0, (0,))
        w_arrived(1, 1)
        w_start(1, 2)
        forward_keys(0, (1,))

    @pl.when(t == 0)
    def _():
        @pl.when(h == 0)
        def _():
            await_keys(0, (0,))

        @pl.when(h > 0)
        def _():
            await_keys(h, (0, 1))

        dk_acc[...] = jnp.zeros_like(dk_acc)
        dv_acc[...] = jnp.zeros_like(dv_acc)
        kt_scr[...] = kv[h, 0].reshape(keys, DH).T

    qs = jnp.concatenate([q_ref[:, g*DH:(g+1)*DH] for g in range(QHEADS)], axis=0)
    k = kv[h, 0].reshape(keys, DH)
    s = lax.dot_general(k, qs, (((1,), (1,)), ((), ())), preferred_element_type=f32)
    top = None
    for n in range(NCTX):
        j = 2 * (n % CHIPS) + n // CHIPS
        part = s[n*T:(n+1)*T]
        if j == 0:
            key = lax.broadcasted_iota(jnp.int32, (T, R), 0)
            token = lax.broadcasted_iota(jnp.int32, (T, R), 1) % T
            part = jnp.where(key <= token, part, -jnp.inf)
        else:
            part = jnp.where(j <= c, part, -jnp.inf)
        s_scr[pl.ds(n*T, T), :] = part
        best = jnp.max(part.reshape(T//8, 8, R), axis=0)
        top = best if top is None else jnp.maximum(top, best)
    top = jnp.max(top, axis=0, keepdims=True)

    @pl.when(step == 0)
    def _():
        await_keys(0, (1,))

    @pl.when(t == 0)
    def _():
        vt_scr[...] = kv[h, 1].reshape(keys, DH).T

    weights = jnp.exp2((s_scr[...] - top) * (scale * LOG2E))
    total = jnp.sum(jnp.sum(weights.reshape(keys//8, 8, R), axis=0), axis=0, keepdims=True)
    wt_scr[...] = weights.astype(bf16)
    acc = jnp.dot(vt_scr[...], wt_scr[...], preferred_element_type=f32)
    inv = 1.0 / total
    out_t = (acc * inv).astype(bf16).astype(f32)
    do_t = jnp.concatenate([do_ref[:, g*DH:(g+1)*DH].astype(f32).T for g in range(QHEADS)], axis=1)
    dos_t = (do_t * inv).astype(bf16).astype(f32)
    delta = jnp.sum(dos_t * out_t, axis=0, keepdims=True)
    dos = jnp.concatenate([dos_t[:, g*DH:(g+1)*DH].T for g in range(QHEADS)], axis=0).astype(bf16)
    for g in range(QHEADS):
        out_ref[:, g*DH:(g+1)*DH] = out_t[:, g*DH:(g+1)*DH].T.astype(bf16)


    @pl.when(step == 1)
    def _():
        project(1)

    @pl.when((t == 0) & (h >= 1))
    def _():
        add_pair(h - 1)

    @pl.when(step == 2)
    def _():
        project(2)

    @pl.when(step == 3)
    def _():
        forward_keys(2)
        project(3)

    @pl.when((t == 0) & (h >= 2))
    def _():
        forward_grads(h - 2)

    @pl.when((t == 1) & (h >= 1))
    def _():
        finish_block(h - 1)

    @pl.when((t == 1) & (h >= 2))
    def _():
        weight_grad(h - 2)

    dprobs = lax.dot_general(kv[h, 1].reshape(keys, DH), dos, (((1,), (1,)), ((), ())), preferred_element_type=f32)
    wb = wt_scr[...]
    ds = (dprobs - delta).astype(bf16) * wb
    dq = jnp.dot(kt_scr[...], ds, preferred_element_type=f32) * scale
    dk_acc[...] += jnp.dot(ds, qs, preferred_element_type=f32)
    dv_acc[...] += jnp.dot(wb, dos, preferred_element_type=f32)
    for g in range(QHEADS):
        dq_ref[:, g*DH:(g+1)*DH] = dq[:, g*DH:(g+1)*DH].T.astype(bf16)

    @pl.when(step == 0)
    def _():
        w_share(1)
        w_arrived(2, 1)
        w_start(2, 2)

    @pl.when(step == 1)
    def _():
        forward_keys(1)
        w_share(2)
        w_arrived(3, 1)
        w_start(3, 2)
        tok_copy.start()
        for j in range(1, GROUP):
            tok_push(j).start()

    @pl.when(step == 2)
    def _():
        w_share(3)

    @pl.when(step == 4)
    def _():
        forward_keys(3)
        tok_copy.wait()
        tok_all().wait_recv()

    @pl.when(t == tiles - 1)
    def _():
        for q in range(CHIPS):
            for parity, ref in ((0, even), (1, odd)):
                rows = pl.ds((CHIPS * parity + q) * T, T)
                ref[h, q, :, :DH] = (dk_acc[rows, :] * scale).astype(bf16)
                ref[h, q, :, DH:] = dv_acc[rows, :].astype(bf16)
        swap(h).start()

    @pl.when((t == tiles - 1) & (h == KVH - 1))
    def _():
        last = KVH - 1
        forward_grads(last - 1)
        add_pair(last)
        weight_grad(last - 1)
        block = weight.shape[4] * weight.shape[5] * weight.shape[6] * weight.shape[7]

        def inputs_part(heads):
            gp = jnp.concatenate([gp_own[2 * hd + u] for hd in heads for u in range(2)], axis=1)
            for n in range(tok_ref.shape[1] // block):
                w = jnp.concatenate([weight[hd, u, n // 2, n % 2].reshape(block, DH)
                                     for hd in heads for u in range(2)], axis=1)
                yield slice(n * block, (n + 1) * block), lax.dot_general(
                    gp, w, (((1,), (1,)), ((), ())), preferred_element_type=f32)

        for columns, part in inputs_part(range(last)):
            gin_acc[:, columns] = part
        finish_block(last)
        for columns, part in inputs_part([last]):
            gin_ref[:, columns] = (gin_acc[:, columns] + part).astype(bf16)
        forward_grads(last)
        weight_grad(last)
        for hd in range(KVH):
            total_w = dw[hd, zh, x, zl].astype(f32)
            dw_all(hd).wait_recv()
            for j in range(1, SPREAD):
                total_w = total_w + dw_landed[hd, j].astype(f32)
            gw_ref[:, hd*DH:(hd+1)*DH] = total_w[:, :DH]
            gw_ref[:, (KVH+hd)*DH:(KVH+hd+1)*DH] = total_w[:, DH:]
        for hd in range(KVH):
            for u in range(2):
                for unit in w_units(hd, u):
                    for phase in range(3):
                        w_three(hd, u, unit, phase).wait_send()
                    w_swap(hd, u, unit).wait_send()
            for us in (((0,), (1,)) if hd == 0 else ((0, 1),)):
                wait_for(CHIPS - 1 - chip, lambda count: kv_some(hd, us, count), "wait_send")
                for k in range(2):
                    @pl.when(core == k)
                    def _():
                        kv_forward(hd, us, k).wait_send()
            wait_for(chip, lambda count: sum_some(hd, count), "wait_send")
            swap(hd).wait_send()
            gp_three(hd).wait_send()
            gp_forward(hd).wait_send()
            dw_all(hd).wait_send()
        tok_all().wait_send()


def main(q, do, tokens, weight, cosine, sine):
    tiles = q.shape[1] // DH // KVH // QHEADS
    keys, R = NCTX * T, QHEADS * T
    tile = pl.BlockSpec((T, R), lambda h, t: (0, h * tiles + t))

    def whole(array):
        return pl.BlockSpec(array.shape, lambda h, t: (0, 0))

    features = tokens.shape[1]
    rows, width = weight.shape
    dma = pltpu.SemaphoreType.DMA
    shared = pltpu.VMEM((KVH, CHIPS, T, 2 * DH), bf16)
    return pl.pallas_call(
        functools.partial(main_kernel, tiles),
        grid=(KVH, tiles),
        in_specs=[tile, tile, whole(tokens), whole(weight), whole(cosine), whole(sine)],
        out_specs=[tile, tile,
                   pl.BlockSpec((T, features), lambda h, t: (0, 0)),
                   pl.BlockSpec((rows, width), lambda h, t: (0, 0))],
        out_shape=[jax.ShapeDtypeStruct(q.shape, bf16), jax.ShapeDtypeStruct(q.shape, bf16),
                   jax.ShapeDtypeStruct((T, features), bf16), jax.ShapeDtypeStruct((rows, width), f32)],
        scratch_shapes=[
            pltpu.VMEM((KVH, 2, 2, CHIPS, T, DH), bf16),
            pltpu.VMEM((keys, R), f32), pltpu.VMEM((keys, R), bf16),
            pltpu.VMEM((DH, keys), bf16), pltpu.VMEM((DH, keys), bf16),
            pltpu.VMEM((keys, DH), f32), pltpu.VMEM((keys, DH), f32),
            shared, shared, shared, shared,
            pltpu.VMEM((T, 2 * DH), f32),
            pltpu.VMEM((KVH, GROUP, T, 2 * DH), bf16),
            pltpu.VMEM((2 * KVH, T, DH), bf16),
            pltpu.VMEM((KVH, 2, 4, 2, 4, 2, 2, rows, DH), bf16),
            pltpu.VMEM((4, 2, 4, 2, 2, rows, T), bf16), pltpu.VMEM((2, 4, 2, rows, GROUP * T), bf16),
            pltpu.VMEM((KVH, 2, 4, 2, rows, 2 * DH), bf16), pltpu.VMEM((KVH, SPREAD, rows, 2 * DH), bf16),
            pltpu.VMEM((T, features), f32),
            dma((30,)), dma((30,)), dma((10,)), dma((10,)), dma,
            dma((KVH + 1,)), dma((KVH + 1,)), dma((KVH + 1,)), dma((KVH + 1,)),
            dma((KVH,)), dma((KVH,)), dma((KVH,)), dma((KVH,)),
            dma((KVH,)), dma((KVH,)), dma((KVH,)), dma((KVH,)),
            dma((KVH,)), dma((KVH,)), dma, dma],
        compiler_params=pltpu.CompilerParams(
            collective_id=0, has_side_effects=True, vmem_limit_bytes=60 * 2**20),
        name="projection_attention_exchanges",
    )(q, do, tokens, weight, cosine, sine)


def copy_kernel(count, *refs):
    sources, results, held, load, store = refs[:count], refs[count:2 * count], refs[2 * count:-2], refs[-2], refs[-1]
    loads, stores = [], []
    for src, dst, mid in zip(sources, results, held):
        rows = min(32, src.shape[0])
        for first in range(0, src.shape[0], rows):
            part = pl.ds(first, rows)
            n = len(loads)
            loads.append(pltpu.make_async_copy(src.at[part], mid.at[part], load.at[n]))
            stores.append(pltpu.make_async_copy(mid.at[part], dst.at[part], store.at[n]))
    for copy in loads:
        copy.start()
    for arrived, copy in zip(loads, stores):
        arrived.wait()
        copy.start()
    for copy in stores:
        copy.wait()


def copy_out(arrays):
    hbm = pl.BlockSpec(memory_space=pl.ANY)
    return pl.pallas_call(
        functools.partial(copy_kernel, len(arrays)),
        in_specs=[hbm] * len(arrays), out_specs=[hbm] * len(arrays),
        out_shape=[jax.ShapeDtypeStruct(a.shape, a.dtype) for a in arrays],
        scratch_shapes=[pltpu.VMEM(a.shape, a.dtype) for a in arrays] + [pltpu.SemaphoreType.DMA((16,))] * 2,
        compiler_params=pltpu.CompilerParams(vmem_limit_bytes=60 * 2**20),
        name="copy_out",
    )(*arrays)


def on_device(inputs, queries, grad_output, kv_weight):
    count = inputs.shape[1]
    ctx = lax.axis_index("ctx")
    cosine, sine = rope_tables(ctx * count + jnp.arange(count, dtype=jnp.int32), DH)
    attn_out, grad_query, grad_inputs, grad_weight = copy_out(main(
        queries[0], grad_output[0], inputs[0], kv_weight,
        jnp.concatenate([cosine, cosine], axis=1), jnp.concatenate([sine, -sine], axis=1)))
    return (attn_out[None], grad_query[None], grad_inputs[None], grad_weight)


def solution(mesh):
    tokens = P("dp", "ctx", None)
    rows = P(("dp", "ctx"), None)
    return jax.shard_map(
        on_device, mesh=mesh, in_specs=(tokens, tokens, tokens, rows),
        out_specs=(tokens, tokens, tokens, rows), check_vma=False)
```

```python
import functools
import math

import jax
import jax.numpy as jnp
from jax import lax
from jax.experimental import pallas as pl
from jax.experimental.pallas import tpu as pltpu
from jax.sharding import PartitionSpec as P

DH = 128
LOG2E = math.log2(math.e)
ROPE_BASE = 500000.0
MESH = pl.DeviceIdType.MESH
NCTX = 16
CHIPS = NCTX // 2
f32, bf16 = jnp.float32, jnp.bfloat16


def rope_tables(positions, head_dim):
    half_dim = head_dim // 2
    frequency = ROPE_BASE ** (-2.0 * jnp.arange(half_dim, dtype=f32) / head_dim)
    angles = positions.astype(f32)[:, None] * frequency[None, :]
    return jnp.cos(angles), jnp.sin(angles)


def position():
    dp, ctx = lax.axis_index("dp"), lax.axis_index("ctx")
    return dp // 2, dp % 2, ctx // 4, (ctx // 2) % 2, ctx % 2


def device_at(y, zh, x, zl, core):
    return (y * 2 + zh, x * 4 + zl * 2 + core)


def meet(peers):
    barrier = pltpu.get_barrier_semaphore()
    for peer in peers:
        pl.semaphore_signal(barrier, inc=1, device_id=peer, device_id_type=MESH)
    pl.semaphore_wait(barrier, len(peers))


QHEADS = 8
GROUP = 8
SPREAD = 16
KVH = 4
T = 128


def main_kernel(tiles, q_ref, do_ref, tok_ref, w_ref, cos_ref, sin_ref,
                out_ref, dq_ref, gin_ref, gw_ref,
                kv, s_scr, wt_scr, kt_scr, vt_scr, dk_acc, dv_acc,
                even, odd, theirs, landed, own32, gp_all, gp_own, weight, tok_own, tok_t, dw, dw_landed, gin_acc,
                w_send, w_recv, ws_send, ws_recv, tok_local, kv_send, kv_recv, fw_send, fw_recv, swap_send, swap_recv, ps_send, ps_recv,
                ag_send, ag_recv, agf_send, agf_recv, dw_send, dw_recv, a_send, a_recv):
    dp, c = lax.axis_index("dp"), lax.axis_index("ctx")
    chip, core = c // 2, c % 2
    partner = (dp, chip * 2 + 1 - core)
    h, t = pl.program_id(0), pl.program_id(1)
    R = QHEADS * T
    keys = NCTX * T
    scale = DH ** -0.5
    far = list(range(1, CHIPS))
    y, zh, x, zl, _ = position()
    z = zh * 2 + zl

    def chip_at(i):
        return (dp, lax.rem(chip + i + CHIPS, CHIPS) * 2 + core)

    def remote(src, dst, send, recv, device):
        return pltpu.make_async_remote_copy(
            src_ref=src, dst_ref=dst, send_sem=send, recv_sem=recv, device_id=device, device_id_type=MESH)

    def w_units(hd, u):
        if hd == 0:
            return ((0, 16, ("zxy", "xyz")[u]), (16, 16, ("yzx", "zxy")[u]))
        return ((0, 32, (("zxy", "yzx"), ("xzy", "yxz"))[hd % 2][u]),)

    def along(axis, step):
        if axis == "x":
            return device_at(y, zh, lax.rem(x + step, 4), zl, core)
        if axis == "y":
            return device_at(lax.rem(y + step, 4), zh, x, zl, core)
        to = lax.rem(z + step, 4)
        return device_at(y, to // 2, x, lax.rem(to, 2), core)

    def w_region(hd, u, unit, phase):
        first, count, axes = unit
        done = axes[:phase]
        yy = slice(None) if "y" in done else y
        xx = slice(None) if "x" in done else x
        zz, zzl = (slice(None), slice(None)) if "z" in done else (zh, zl)
        return weight.at[hd, u, yy, zz, xx, zzl, core, pl.ds(first, count)]

    def w_number(hd, u, unit):
        return 2 * u + unit[0] // 16 if hd == 0 else 2 + 2 * hd + u

    def w_push(hd, u, unit, phase, step):
        region = w_region(hd, u, unit, phase)
        n = w_number(hd, u, unit) * 3 + phase
        return remote(region, region, w_send.at[n], w_recv.at[n], along(unit[2][phase], step))

    def w_three(hd, u, unit, phase):
        first, count, _ = unit
        rest = ((0, 0, 0), (0, slice(None), 0), (slice(None), slice(None), slice(None)))[phase]
        region = weight.at[(hd, u, pl.ds(0, 3)) + rest + (core, pl.ds(first, count))]
        n = w_number(hd, u, unit) * 3 + phase
        return remote(region, region, w_send.at[n], w_recv.at[n], partner)

    def w_start(hd, phase, us=(0, 1)):
        for u in us:
            for unit in w_units(hd, u):
                for step in (2, 1, 3):
                    w_push(hd, u, unit, phase, step).start()

    def w_arrived(hd, phase, us=(0, 1)):
        for u in us:
            for unit in w_units(hd, u):
                w_three(hd, u, unit, phase).wait_recv()

    def w_swap(hd, u, unit):
        region = w_region(hd, u, unit, 3)
        n = w_number(hd, u, unit)
        return remote(region, region, ws_send.at[n], ws_recv.at[n], partner)

    def w_share(hd, us=(0, 1)):
        for u in us:
            for unit in w_units(hd, u):
                w_three(hd, u, unit, 2).wait_recv()
                w_swap(hd, u, unit).start()

    def project(hd, us=(0, 1)):
        for u in us:
            for unit in w_units(hd, u):
                w_swap(hd, u, unit).wait_recv()
            part = jnp.dot(tok_ref[...], weight[hd, u].reshape(tok_ref.shape[1], DH), preferred_element_type=f32)
            if u == 0:
                part = part * cos_ref[...] - pltpu.roll(part, DH // 2, 1) * sin_ref[...]
            kv[hd, u, 0, 0] = part.astype(bf16)
        for i in far:
            @pl.when(chip + i < CHIPS)
            def _():
                kv_push(hd, us, i).start()

    def wait_for(n, stand_in, way):
        for count in far:
            @pl.when(n == count)
            def _():
                getattr(stand_in(count), way)()

    def kv_part(hd, us):
        return hd + 1 if len(us) == 2 else us[0]

    def kv_at(hd, us, parity, slots):
        return kv.at[hd, pl.ds(us[0], len(us)), parity, slots]

    def kv_push(hd, us, i):
        n = kv_part(hd, us)
        return remote(kv_at(hd, us, 0, 0), kv_at(hd, us, 0, i), kv_send.at[n], kv_recv.at[n], chip_at(i))

    def kv_some(hd, us, count):
        n = kv_part(hd, us)
        region = kv_at(hd, us, 0, pl.ds(1, count))
        return remote(region, region, kv_send.at[n], kv_recv.at[n], partner)

    def kv_forward(hd, us, from_core):
        n = kv_part(hd, us)
        here, there = (pl.ds(0, 8), pl.ds(0, 8)) if from_core == 0 else (pl.ds(1, 7), pl.ds(0, 7))
        return remote(kv_at(hd, us, 0, here), kv_at(hd, us, 1, there), fw_send.at[n], fw_recv.at[n], partner)

    def swap(hd):
        return remote(odd.at[hd], theirs.at[hd], swap_send.at[hd], swap_recv.at[hd], partner)

    def sum_push(hd, i):
        return remote(even.at[hd, i], landed.at[hd, i], ps_send.at[hd], ps_recv.at[hd], chip_at(-i))

    def sum_some(hd, count):
        region = landed.at[hd, pl.ds(1, count)]
        return remote(region, region, ps_send.at[hd], ps_recv.at[hd], partner)

    def gp_push(hd, dy):
        return remote(gp_all.at[hd, 0], gp_all.at[hd, dy], ag_send.at[hd], ag_recv.at[hd], along("y", dy))

    def gp_three(hd):
        region = gp_all.at[hd, pl.ds(1, 3)]
        return remote(region, region, ag_send.at[hd], ag_recv.at[hd], partner)

    def gp_forward(hd):
        return remote(gp_all.at[hd, pl.ds(0, 4)], gp_all.at[hd, pl.ds(4, 4)],
                      agf_send.at[hd], agf_recv.at[hd], partner)

    def tok_push(j):
        to_y, to_core = lax.rem(y + j % 4, 4), lax.rem(core + j // 4, 2)
        return remote(tok_own.at[to_y, :, :, :, to_core], tok_t.at[:, :, :, :, pl.ds(j * T, T)],
                      a_send, a_recv, device_at(to_y, zh, x, zl, to_core))

    def tok_all():
        region = tok_t.at[:, :, :, :, pl.ds(T, (GROUP - 1) * T)]
        return remote(region, region, a_send, a_recv, partner)

    def across(j):
        to = lax.rem(z + j % 4, 4)
        return to // 2, lax.rem(x + j // 4, 4), lax.rem(to, 2)

    def dw_push(group, j):
        to_zh, to_x, to_zl = across(j)
        heads = pl.ds(*((0, 2), (2, 1), (3, 1))[group])
        return remote(dw.at[to_zh, to_x, to_zl, heads], dw_landed.at[j, heads], dw_send.at[group], dw_recv.at[group],
                      device_at(y, to_zh, to_x, to_zl, core))

    def dw_all(group):
        region = dw_landed.at[pl.ds(1, SPREAD - 1), pl.ds(*((0, 2), (2, 1), (3, 1))[group])]
        return remote(region, region, dw_send.at[group], dw_recv.at[group], partner)

    tok_copy = pltpu.make_async_copy(tok_own.at[y, :, :, :, core], tok_t.at[:, :, :, :, pl.ds(0, T)], tok_local)

    def forward_keys(hd, us=(0, 1)):
        wait_for(chip, lambda count: kv_some(hd, us, count), "wait_recv")
        for k in range(2):
            @pl.when(core == k)
            def _():
                kv_forward(hd, us, k).start()

    def await_keys(hd, us):
        for k in range(2):
            @pl.when(core == k)
            def _():
                kv_forward(hd, us, 1 - k).wait_recv()

    def add_pair(hd):
        swap(hd).wait_recv()
        own32[...] = even[hd, 0].astype(f32) + theirs[hd, lax.rem(CHIPS - core, CHIPS)].astype(f32)
        for i in far:
            @pl.when(i <= chip)
            def _():
                total = even[hd, i].astype(f32) + theirs[hd, i - core].astype(f32)
                even[hd, i] = total.astype(bf16)
                sum_push(hd, i).start()

    def finish_block(hd):
        wait_for(CHIPS - 1 - chip, lambda count: sum_some(hd, count), "wait_recv")
        for i in far:
            @pl.when(chip + i < CHIPS)
            def _():
                own32[...] += landed[hd, i].astype(f32)
        key_part = own32[:, :DH]
        key_part = (key_part * cos_ref[...] + pltpu.roll(key_part, DH // 2, 1) * sin_ref[...]).astype(bf16)
        value_part = own32[:, DH:].astype(bf16)
        gp_all[hd, 0, :, :DH] = key_part
        gp_all[hd, 0, :, DH:] = value_part
        gp_own[2 * hd] = key_part
        gp_own[2 * hd + 1] = value_part
        for dy in (1, 2, 3):
            gp_push(hd, dy).start()

    def forward_grads(hd):
        gp_three(hd).wait_recv()
        gp_forward(hd).start()

    def weight_grad(hd):
        gp_forward(hd).wait_recv()
        part = jnp.dot(tok_t[...].reshape(-1, GROUP * T), gp_all[hd].reshape(GROUP * T, 2 * DH),
                       preferred_element_type=f32)
        dw[:, :, :, hd] = part.reshape(dw.shape[:3] + dw.shape[4:]).astype(bf16)

    def spread(group):
        for j in range(1, SPREAD):
            dw_push(group, j).start()

    step = h * tiles + t

    @pl.when((h == 0) & (t == 0))
    def _():
        meet([partner] + [along(axis, k) for axis in "xyz" for k in (1, 2, 3)])
        for hd in range(KVH):
            for u in range(2):
                first = (u * KVH + hd) * DH
                weight[hd, u, y, zh, x, zl, core] = w_ref[:, first:first + DH]
        for u in range(2):
            w_start(0, 0, (u,))
        for phase in range(2):
            for u in range(2):
                w_arrived(0, phase, (u,))
                w_start(0, phase + 1, (u,))
        for hd in range(1, KVH):
            w_start(hd, 0)
        rows = tok_own.shape[5]
        for n in range(tok_ref.shape[1] // T):
            turned = tok_ref[:, n*T:(n+1)*T].T
            for m in range(T // rows):
                g = n * (T // rows) + m
                tok_own[g // 32, g // 16 % 2, g // 4 % 4, g // 2 % 2, g % 2] = turned[m*rows:(m+1)*rows]
        w_share(0, (0,))
        w_share(0, (1,))
        project(0, (0,))
        project(0, (1,))
        for hd in range(1, KVH):
            w_arrived(hd, 0)
            w_start(hd, 1)
        for i in far:
            @pl.when(i > chip)
            def _():
                kv[:, :, 0, i] = jnp.zeros((KVH, 2, T, DH), bf16)

        @pl.when(core == 0)
        def _():
            kv[:, :, 1, CHIPS - 1] = jnp.zeros((KVH, 2, T, DH), bf16)

        forward_keys(0, (0,))
        w_arrived(1, 1)
        w_start(1, 2)
        forward_keys(0, (1,))

    @pl.when(t == 0)
    def _():
        @pl.when(h == 0)
        def _():
            await_keys(0, (0,))

        @pl.when(h > 0)
        def _():
            await_keys(h, (0, 1))

        dk_acc[...] = jnp.zeros_like(dk_acc)
        dv_acc[...] = jnp.zeros_like(dv_acc)
        kt_scr[...] = kv[h, 0].reshape(keys, DH).T

    qs = jnp.concatenate([q_ref[:, g*DH:(g+1)*DH] for g in range(QHEADS)], axis=0)
    k = kv[h, 0].reshape(keys, DH)
    s = lax.dot_general(k, qs, (((1,), (1,)), ((), ())), preferred_element_type=f32)
    top = None
    for n in range(NCTX):
        j = 2 * (n % CHIPS) + n // CHIPS
        part = s[n*T:(n+1)*T]
        if j == 0:
            key = lax.broadcasted_iota(jnp.int32, (T, R), 0)
            token = lax.broadcasted_iota(jnp.int32, (T, R), 1) % T
            part = jnp.where(key <= token, part, -jnp.inf)
        else:
            part = jnp.where(j <= c, part, -jnp.inf)
        s_scr[pl.ds(n*T, T), :] = part
        best = jnp.max(part.reshape(T//8, 8, R), axis=0)
        top = best if top is None else jnp.maximum(top, best)
    top = jnp.max(top, axis=0, keepdims=True)

    @pl.when(step == 0)
    def _():
        await_keys(0, (1,))

    @pl.when(t == 0)
    def _():
        vt_scr[...] = kv[h, 1].reshape(keys, DH).T

    weights = jnp.exp2((s_scr[...] - top) * (scale * LOG2E))
    total = jnp.sum(jnp.sum(weights.reshape(keys//8, 8, R), axis=0), axis=0, keepdims=True)
    wt_scr[...] = weights.astype(bf16)
    acc = jnp.dot(vt_scr[...], wt_scr[...], preferred_element_type=f32)
    inv = 1.0 / total
    out_t = (acc * inv).astype(bf16).astype(f32)
    do_t = jnp.concatenate([do_ref[:, g*DH:(g+1)*DH].astype(f32).T for g in range(QHEADS)], axis=1)
    dos_t = (do_t * inv).astype(bf16).astype(f32)
    delta = jnp.sum(dos_t * out_t, axis=0, keepdims=True)
    dos = jnp.concatenate([dos_t[:, g*DH:(g+1)*DH].T for g in range(QHEADS)], axis=0).astype(bf16)
    for g in range(QHEADS):
        out_ref[:, g*DH:(g+1)*DH] = out_t[:, g*DH:(g+1)*DH].T.astype(bf16)


    @pl.when(step == 1)
    def _():
        project(1)

    @pl.when((t == 0) & (h >= 1))
    def _():
        add_pair(h - 1)

    @pl.when(step == 2)
    def _():
        project(2)

    @pl.when(step == 3)
    def _():
        forward_keys(2)
        project(3)

    @pl.when((t == 0) & (h >= 2))
    def _():
        forward_grads(h - 2)

    @pl.when((t == 1) & (h >= 1))
    def _():
        finish_block(h - 1)

    @pl.when((t == 1) & (h >= 2))
    def _():
        weight_grad(h - 2)

    @pl.when(step == 2 * KVH - 1)
    def _():
        spread(0)

    dprobs = lax.dot_general(kv[h, 1].reshape(keys, DH), dos, (((1,), (1,)), ((), ())), preferred_element_type=f32)
    wb = wt_scr[...]
    ds = (dprobs - delta).astype(bf16) * wb
    dq = jnp.dot(kt_scr[...], ds, preferred_element_type=f32) * scale
    dk_acc[...] += jnp.dot(ds, qs, preferred_element_type=f32)
    dv_acc[...] += jnp.dot(wb, dos, preferred_element_type=f32)
    for g in range(QHEADS):
        dq_ref[:, g*DH:(g+1)*DH] = dq[:, g*DH:(g+1)*DH].T.astype(bf16)

    @pl.when(step == 0)
    def _():
        w_share(1)
        w_arrived(2, 1)
        w_start(2, 2)

    @pl.when(step == 1)
    def _():
        forward_keys(1)
        w_share(2)
        w_arrived(3, 1)
        w_start(3, 2)
        tok_copy.start()
        for j in range(1, GROUP):
            tok_push(j).start()

    @pl.when(step == 2)
    def _():
        w_share(3)

    @pl.when(step == 4)
    def _():
        forward_keys(3)
        tok_copy.wait()
        tok_all().wait_recv()

    @pl.when(t == tiles - 1)
    def _():
        for parity, ref in ((1, odd), (0, even)):
            for q in range(CHIPS):
                rows = pl.ds((CHIPS * parity + q) * T, T)
                ref[h, q, :, :DH] = (dk_acc[rows, :] * scale).astype(bf16)
                ref[h, q, :, DH:] = dv_acc[rows, :].astype(bf16)
            if parity == 1:
                swap(h).start()

    @pl.when((t == tiles - 1) & (h == KVH - 1))
    def _():
        last = KVH - 1
        add_pair(last)
        forward_grads(last - 1)
        block = weight.shape[4] * weight.shape[5] * weight.shape[6] * weight.shape[7]

        def inputs_part(heads):
            gp = jnp.concatenate([gp_own[2 * hd + u] for hd in heads for u in range(2)], axis=1)
            for n in range(tok_ref.shape[1] // block):
                w = jnp.concatenate([weight[hd, u, n // 2, n % 2].reshape(block, DH)
                                     for hd in heads for u in range(2)], axis=1)
                yield slice(n * block, (n + 1) * block), lax.dot_general(
                    gp, w, (((1,), (1,)), ((), ())), preferred_element_type=f32)

        for columns, part in inputs_part(range(last)):
            gin_acc[:, columns] = part
        finish_block(last)
        weight_grad(last - 1)
        spread(1)
        for columns, part in inputs_part([last]):
            gin_ref[:, columns] = (gin_acc[:, columns] + part).astype(bf16)
        forward_grads(last)
        weight_grad(last)
        spread(2)
        for hd in range(KVH):
            total_w = dw[zh, x, zl, hd].astype(f32)
            if hd != 1:
                dw_all(max(hd - 1, 0)).wait_recv()
            for j in range(1, SPREAD):
                total_w = total_w + dw_landed[j, hd].astype(f32)
            gw_ref[:, hd*DH:(hd+1)*DH] = total_w[:, :DH]
            gw_ref[:, (KVH+hd)*DH:(KVH+hd+1)*DH] = total_w[:, DH:]
        for hd in range(KVH):
            for u in range(2):
                for unit in w_units(hd, u):
                    for phase in range(3):
                        w_three(hd, u, unit, phase).wait_send()
                    w_swap(hd, u, unit).wait_send()
            for us in (((0,), (1,)) if hd == 0 else ((0, 1),)):
                wait_for(CHIPS - 1 - chip, lambda count: kv_some(hd, us, count), "wait_send")
                for k in range(2):
                    @pl.when(core == k)
                    def _():
                        kv_forward(hd, us, k).wait_send()
            wait_for(chip, lambda count: sum_some(hd, count), "wait_send")
            swap(hd).wait_send()
            gp_three(hd).wait_send()
            gp_forward(hd).wait_send()
            if hd != 1:
                dw_all(max(hd - 1, 0)).wait_send()
        tok_all().wait_send()


def main(q, do, tokens, weight, cosine, sine):
    tiles = q.shape[1] // DH // KVH // QHEADS
    keys, R = NCTX * T, QHEADS * T
    tile = pl.BlockSpec((T, R), lambda h, t: (0, h * tiles + t))

    def whole(array):
        return pl.BlockSpec(array.shape, lambda h, t: (0, 0))

    features = tokens.shape[1]
    rows, width = weight.shape
    dma = pltpu.SemaphoreType.DMA
    shared = pltpu.VMEM((KVH, CHIPS, T, 2 * DH), bf16)
    return pl.pallas_call(
        functools.partial(main_kernel, tiles),
        grid=(KVH, tiles),
        in_specs=[tile, tile, whole(tokens), whole(weight), whole(cosine), whole(sine)],
        out_specs=[tile, tile,
                   pl.BlockSpec((T, features), lambda h, t: (0, 0)),
                   pl.BlockSpec((rows, width), lambda h, t: (0, 0))],
        out_shape=[jax.ShapeDtypeStruct(q.shape, bf16), jax.ShapeDtypeStruct(q.shape, bf16),
                   jax.ShapeDtypeStruct((T, features), bf16), jax.ShapeDtypeStruct((rows, width), f32)],
        scratch_shapes=[
            pltpu.VMEM((KVH, 2, 2, CHIPS, T, DH), bf16),
            pltpu.VMEM((keys, R), f32), pltpu.VMEM((keys, R), bf16),
            pltpu.VMEM((DH, keys), bf16), pltpu.VMEM((DH, keys), bf16),
            pltpu.VMEM((keys, DH), f32), pltpu.VMEM((keys, DH), f32),
            shared, shared, shared, shared,
            pltpu.VMEM((T, 2 * DH), f32),
            pltpu.VMEM((KVH, GROUP, T, 2 * DH), bf16),
            pltpu.VMEM((2 * KVH, T, DH), bf16),
            pltpu.VMEM((KVH, 2, 4, 2, 4, 2, 2, rows, DH), bf16),
            pltpu.VMEM((4, 2, 4, 2, 2, rows, T), bf16), pltpu.VMEM((2, 4, 2, rows, GROUP * T), bf16),
            pltpu.VMEM((2, 4, 2, KVH, rows, 2 * DH), bf16), pltpu.VMEM((SPREAD, KVH, rows, 2 * DH), bf16),
            pltpu.VMEM((T, features), f32),
            dma((30,)), dma((30,)), dma((10,)), dma((10,)), dma,
            dma((KVH + 1,)), dma((KVH + 1,)), dma((KVH + 1,)), dma((KVH + 1,)),
            dma((KVH,)), dma((KVH,)), dma((KVH,)), dma((KVH,)),
            dma((KVH,)), dma((KVH,)), dma((KVH,)), dma((KVH,)),
            dma((KVH,)), dma((KVH,)), dma, dma],
        compiler_params=pltpu.CompilerParams(
            collective_id=0, has_side_effects=True, vmem_limit_bytes=60 * 2**20),
        name="projection_attention_exchanges",
    )(q, do, tokens, weight, cosine, sine)


def copy_kernel(count, *refs):
    sources, results, held, load, store = refs[:count], refs[count:2 * count], refs[2 * count:-2], refs[-2], refs[-1]
    loads, stores = [], []
    for src, dst, mid in zip(sources, results, held):
        rows = min(32, src.shape[0])
        for first in range(0, src.shape[0], rows):
            part = pl.ds(first, rows)
            n = len(loads)
            loads.append(pltpu.make_async_copy(src.at[part], mid.at[part], load.at[n]))
            stores.append(pltpu.make_async_copy(mid.at[part], dst.at[part], store.at[n]))
    for copy in loads:
        copy.start()
    for arrived, copy in zip(loads, stores):
        arrived.wait()
        copy.start()
    for copy in stores:
        copy.wait()


def copy_out(arrays):
    hbm = pl.BlockSpec(memory_space=pl.ANY)
    return pl.pallas_call(
        functools.partial(copy_kernel, len(arrays)),
        in_specs=[hbm] * len(arrays), out_specs=[hbm] * len(arrays),
        out_shape=[jax.ShapeDtypeStruct(a.shape, a.dtype) for a in arrays],
        scratch_shapes=[pltpu.VMEM(a.shape, a.dtype) for a in arrays] + [pltpu.SemaphoreType.DMA((16,))] * 2,
        compiler_params=pltpu.CompilerParams(vmem_limit_bytes=60 * 2**20),
        name="copy_out",
    )(*arrays)


def on_device(inputs, queries, grad_output, kv_weight):
    count = inputs.shape[1]
    ctx = lax.axis_index("ctx")
    cosine, sine = rope_tables(ctx * count + jnp.arange(count, dtype=jnp.int32), DH)
    attn_out, grad_query, grad_inputs, grad_weight = copy_out(main(
        queries[0], grad_output[0], inputs[0], kv_weight,
        jnp.concatenate([cosine, cosine], axis=1), jnp.concatenate([sine, -sine], axis=1)))
    return (attn_out[None], grad_query[None], grad_inputs[None], grad_weight)


def solution(mesh):
    tokens = P("dp", "ctx", None)
    rows = P(("dp", "ctx"), None)
    return jax.shard_map(
        on_device, mesh=mesh, in_specs=(tokens, tokens, tokens, rows),
        out_specs=(tokens, tokens, tokens, rows), check_vma=False)
```
